512 devices in a mesh: role: 8 (over z_lo, core), fsdp: 64 (over z_hi, y, x).
Axes of the slice: x: 4, y: 4, z: 16 (z_hi: 4, z_lo: 4; z = z_hi * 4 + z_lo), core: 2. Of those that a mesh axis runs over, the one named last changes fastest.
Arguments:
- teacher_hidden: bfloat16 [8192, 16384], P('fsdp', 'role'), may hold values from -28 to 28
- teacher_head: bfloat16 [16384, 2048], P(('role', 'fsdp')), may hold values from -0.25 to 0.25
- student_hidden: bfloat16 [8192, 4096], P('fsdp', 'role'), may hold values from -28 to 28
- student_head: bfloat16 [4096, 2048], P(('role', 'fsdp')), may hold values from -0.5 to 0.5
- teacher_rest: float32 [8192], P('fsdp'), may hold values from 6 to 14
- student_rest: float32 [8192], P('fsdp'), may hold values from 6 to 14
Outputs:
- kl_loss: float32 [8192], P('fsdp')
- grad_head: float32 [4096, 2048], P(('role', 'fsdp'))
- grad_hidden: float32 [8192, 4096], P('fsdp', 'role')
The draws below stay inside these ranges and needn't reach their ends.
All inputs are finite; a program needn't handle non-finite values.
Results may differ from the reference program's by a relative error of at most 0.003.
Values may be sent and summed in bfloat16 or wider, within the bound.
A program may use at most 64 MiB of HBM per device.

```python
import jax
import jax.numpy as jnp

DT = 16384
DS = 4096
V = 2048
TOKENS = 8192


def hidden_states(key, width):
    first = jax.random.fold_in(key, 0)
    values = jnp.clip(jax.random.normal(first, (TOKENS, width), jnp.float32), -5.0, 5.0)
    return values.astype(jnp.bfloat16)


def draw_teacher_hidden(key, part):
    key = jax.random.fold_in(key, 11)
    return hidden_states(key, DT)


def draw_student_hidden(key, part):
    key = jax.random.fold_in(key, 23)
    return hidden_states(key, DS)


def level_of(own_key, dims, cuts, low, high):
    def one(dim, shards_of):
        heights = jax.random.uniform(jax.random.fold_in(jax.random.fold_in(own_key, 6), dim), (shards_of,), jnp.float32, low / len(cuts), high / len(cuts))
        return jnp.repeat(jnp.exp(heights), dims[dim] // shards_of).reshape((-1,) + (1,) * (len(dims) - dim - 1))

    level = one(*cuts[0])
    for cut in cuts[1:]:
        level = level * one(*cut)
    return level


def normal_values(own_key, dims, scale, reach, pieces=(), held_as=jnp.bfloat16):
    values = jax.random.normal(own_key, dims, jnp.float32) * scale
    if len(pieces) > 0:
        values = level_of(own_key, dims, pieces, -0.22, 0.18) * values
    return jnp.clip(values, min=-reach, max=reach).astype(held_as)


def setup_inputs(seed: int = 0) -> dict:
    key_of = jax.random.split(jax.random.key(seed), 7)
    return {
        "teacher_hidden": draw_teacher_hidden(jax.random.fold_in(key_of[6], 71), 0),
        "teacher_head": normal_values(key_of[1], (DT, V), (DT // 36) ** -0.5, 0.25, ((0, 512),)),
        "student_hidden": draw_student_hidden(jax.random.fold_in(key_of[6], 71), 0),
        "student_head": normal_values(key_of[3], (DS, V), (DS // 36) ** -0.5, 0.5, ((0, 512),)),
        "teacher_rest": jnp.clip(6.0 + 8.0 * jax.random.uniform(key_of[4], (TOKENS,), jnp.float32) ** level_of(key_of[4], (TOKENS,), ((0, 64),), -0.2, 0.2), 6.0, 14.0),
        "student_rest": jnp.clip(6.0 + 8.0 * jax.random.uniform(key_of[5], (TOKENS,), jnp.float32) ** level_of(key_of[5], (TOKENS,), ((0, 64),), -0.2, 0.2), 6.0, 14.0),
    }


def log_normalize(scaled, rest):
    top = jnp.max(scaled, axis=-1, keepdims=True)
    local = top + jnp.log(jnp.sum(jnp.exp(scaled - top), axis=-1, keepdims=True))
    return scaled - jnp.logaddexp(local, rest[:, None])


def distill(teacher_logits, student_logits, teacher_rest, student_rest):
    log_teacher = log_normalize(teacher_logits / 2.0, teacher_rest)
    log_student = log_normalize(student_logits / 2.0, student_rest)
    prob_teacher = jnp.exp(log_teacher)
    prob_student = jnp.exp(log_student)
    kl_loss = 16.0 * jnp.sum(prob_teacher * (log_teacher - log_student), axis=-1)
    grad_logits = (8.0 * (prob_student - prob_teacher)).astype(jnp.bfloat16)
    return kl_loss, grad_logits


def reference(teacher_hidden, teacher_head, student_hidden, student_head, teacher_rest, student_rest):
    teacher_logits = jnp.dot(teacher_hidden, teacher_head, preferred_element_type=jnp.float32)
    student_logits = jnp.dot(student_hidden, student_head, preferred_element_type=jnp.float32)
    kl_loss, grad_logits = distill(teacher_logits, student_logits, teacher_rest, student_rest)
    grad_head = jnp.dot(student_hidden.T, grad_logits, preferred_element_type=jnp.float32)
    grad_hidden = jnp.dot(grad_logits, student_head.T, preferred_element_type=jnp.float32)
    return kl_loss, grad_head, grad_hidden
```

```python
import jax
import jax.numpy as jnp
from jax import lax
from jax.experimental import pallas as pl
from jax.experimental.pallas import tpu as pltpu
from jax.sharding import PartitionSpec as P

MESH = pl.DeviceIdType.MESH
F32 = jnp.float32
BF16 = jnp.bfloat16
N_COPY = 112


def mod4(v):
    return lax.rem(v + 8, 4)


def distill_kernel(
    at_hbm,
    bt_hbm,
    as_hbm,
    sh_ref,
    tr_ref,
    sr_ref,
    kl_out,
    gw_out,
    gh_out,
    bs_src,
    rest_src,
    at_buf,
    as_buf,
    bt_buf,
    bs_buf,
    bs_full,
    as_t,
    rest_buf,
    ct_send,
    ct_recv,
    ct_own,
    cs_send,
    cs_recv,
    cs_own,
    zt_recv,
    zs_recv,
    stat_buf,
    g_buf,
    kl_buf,
    gh_own,
    gh_send,
    gh_recv,
    gw_own,
    gw_send,
    gw_recv,
    w2_send,
    w2_recv,
    send_sem,
    recv_sem,
    local_sem,
):
    role = lax.axis_index("role")
    fsdp = lax.axis_index("fsdp")
    zl, c = lax.div(role, 2), lax.rem(role, 2)
    zh, y, x = lax.div(fsdp, 16), lax.rem(lax.div(fsdp, 4), 4), lax.rem(fsdp, 4)

    def dev(dzl=0, dc=0, dzh=0, dy=0, dx=0):
        r = mod4(zl + dzl) * 2 + lax.rem(c + dc, 2)
        f = (mod4(zh + dzh) * 4 + mod4(y + dy)) * 4 + mod4(x + dx)
        return (r, f)

    started = []

    def send(src, dst, to):
        k = len(started)
        copy = pltpu.make_async_remote_copy(
            src_ref=src,
            dst_ref=dst,
            send_sem=send_sem.at[k],
            recv_sem=recv_sem.at[k],
            device_id=to,
            device_id_type=MESH,
        )
        copy.start()
        started.append(copy)
        return copy

    def arrive(*copies):
        for copy in copies:
            copy.wait_recv()

    partners = [dev(dzh=a, dx=b) for a in range(4) for b in range(4) if a + b > 0]
    partners += [dev(dy=d) for d in (1, 2, 3)]
    partners += [dev(dzl=a, dc=b) for a in range(4) for b in range(2) if a + b > 0]
    barrier = pltpu.get_barrier_semaphore()
    for to in partners:
        pl.semaphore_signal(barrier, inc=1, device_id=to, device_id_type=MESH)

    own_at = pltpu.make_async_copy(at_hbm, at_buf.at[x], local_sem.at[0])
    own_as = pltpu.make_async_copy(as_hbm, as_buf.at[x], local_sem.at[1])
    piece = zh * 4 + y
    row32 = pl.multiple_of(x * 32, 32)
    row16 = pl.multiple_of(x * 16, 16)
    own_bt = pltpu.make_async_copy(
        bt_hbm.at[:, pl.ds(pl.multiple_of(x * 512, 512), 512)],
        bt_buf.at[piece, pl.ds(row32, 32)],
        local_sem.at[2],
    )
    own_as.start()
    own_bt.start()
    own_at.start()

    for q in range(4):
        wide = sh_ref[:, q * 512 : (q + 1) * 512].astype(F32)
        bs_src[q] = jnp.concatenate([wide[:, :256], wide[:, 256:]], axis=0).astype(BF16)
    bs_buf[piece, pl.ds(row16, 16)] = bs_src[x]
    r8 = lax.broadcasted_iota(jnp.int32, (8, 128), 0)
    rest = jnp.where(r8 == 0, tr_ref[...], jnp.where(r8 == 1, sr_ref[...], 0.0))
    rest_src[...] = rest
    rest_buf[x] = rest

    pl.semaphore_wait(barrier, len(partners))

    bs_a2a, bt_a2a = [], []
    for d in (1, 3, 2):
        q = mod4(x + d)
        bs_a2a.append(send(bs_src.at[q], bs_buf.at[piece, pl.ds(row16, 16)], dev(dx=d)))
    for d in (1, 3, 2):
        q = mod4(x + d)
        bt_a2a.append(
            send(
                bt_hbm.at[:, pl.ds(pl.multiple_of(q * 512, 512), 512)],
                bt_buf.at[piece, pl.ds(row32, 32)],
                dev(dx=d),
            )
        )
    as_1 = [send(as_hbm, as_buf.at[x], dev(dx=d)) for d in (1, 3)]
    rests = [send(rest_src, rest_buf.at[x], dev(dx=d)) for d in (1, 3, 2)]
    at_1 = [send(at_hbm, at_buf.at[x], dev(dx=d)) for d in (1, 3)]

    def halves(buf, i, rows):
        return buf.at[i, pl.ds(0, rows)], buf.at[i, pl.ds(rows, rows)]

    def forward_x(first, buf):
        arrive(first[0])
        lo = halves(buf, mod4(x - 1), 64)[0]
        a = send(lo, lo, dev(dx=1))
        arrive(first[1])
        hi = halves(buf, mod4(x + 1), 64)[1]
        b = send(hi, hi, dev(dx=3))
        return [a, b]

    def both_y(buf, i):
        return [send(buf.at[i], buf.at[i], dev(dy=d)) for d in (1, 3)]

    def both_z(buf):
        return [send(buf.at[piece], buf.at[piece], dev(dzh=d)) for d in (1, 3)]

    def forward_z(first, buf, rows):
        arrive(first[0])
        i = mod4(zh - 1) * 4 + y
        lo = halves(buf, i, rows)[0]
        a = send(lo, lo, dev(dzh=1))
        ya = both_y(buf, i)
        arrive(first[1])
        i = mod4(zh + 1) * 4 + y
        hi = halves(buf, i, rows)[1]
        b = send(hi, hi, dev(dzh=3))
        yb = both_y(buf, i)
        return [a, b], ya, yb

    def forward_y(first, buf, zi, rows):
        arrive(first[0])
        lo = halves(buf, zi * 4 + mod4(y - 1), rows)[0]
        a = send(lo, lo, dev(dy=1))
        arrive(first[1])
        hi = halves(buf, zi * 4 + mod4(y + 1), rows)[1]
        b = send(hi, hi, dev(dy=3))
        return [a, b]

    prev, nxt, far = mod4(zh - 1), mod4(zh + 1), mod4(zh + 2)

    arrive(*bs_a2a)
    bs_z = both_z(bs_buf)
    bs_y0 = both_y(bs_buf, piece)
    own_bt.wait()
    arrive(*bt_a2a)
    bt_z = both_z(bt_buf)
    bt_y0 = both_y(bt_buf, piece)

    as_2 = forward_x(as_1, as_buf)
    bs_z2, bs_y1, bs_y2 = forward_z(bs_z, bs_buf, 32)
    bs_f0 = forward_y(bs_y0, bs_buf, zh, 32)
    bt_f0 = forward_y(bt_y0, bt_buf, zh, 64)
    bs_f1 = forward_y(bs_y1, bs_buf, prev, 32)
    bs_f2 = forward_y(bs_y2, bs_buf, nxt, 32)
    arrive(*bs_z2)
    bs_y3 = both_y(bs_buf, far * 4 + y)

    own_as.wait()
    arrive(*as_2)

    def turn(i, carry):
        cols = pl.ds(pl.multiple_of(i * 128, 128), 128)
        block = as_buf[:, :, cols].reshape(512, 128).astype(F32)
        flat = block.T.astype(BF16)
        for yy in range(4):
            at = pl.multiple_of((yy * 4 + i) * 32, 32)
            as_t[pl.ds(at, 32)] = flat[yy * 32 : (yy + 1) * 32]
        return carry

    lax.fori_loop(0, 4, turn, 0)

    bs_f3 = forward_y(bs_y3, bs_buf, far, 32)
    arrive(*bs_f0, *bs_f1, *bs_f2, *bs_f3)
    for i in range(16):
        tall = bs_buf[i].astype(F32).reshape(4, 2, 8, 256)
        rows = slice(i * 32, (i + 1) * 32)
        bs_full[rows, :256] = tall[:, 0].reshape(32, 256).astype(BF16)
        bs_full[rows, 256:] = tall[:, 1].reshape(32, 256).astype(BF16)

    def logits(a_buf, b_of, out, half):
        a = a_buf[pl.ds(half * 2, 2)]
        a = a.reshape(256, a.shape[-1])

        def column(i, carry):
            cols = pl.ds(pl.multiple_of(i * 256, 256), 256)
            out[:, cols] = jnp.dot(a, b_of(cols), preferred_element_type=F32)
            return carry

        lax.fori_loop(0, 2, column, 0)

    def student_b(cols):
        return bs_full[:, cols]

    logits(as_buf, student_b, cs_send, 1 - c)
    cs_swap = send(cs_send, cs_recv, dev(dc=1))
    logits(as_buf, student_b, cs_own, c)

    at_2 = forward_x(at_1, at_buf)
    bt_z2, bt_y1, bt_y2 = forward_z(bt_z, bt_buf, 64)
    bt_f1 = forward_y(bt_y1, bt_buf, prev, 64)
    bt_f2 = forward_y(bt_y2, bt_buf, nxt, 64)
    arrive(*bt_z2)
    bt_y3 = both_y(bt_buf, far * 4 + y)

    def scatter_z(swap, own, recv, zrecv):
        arrive(swap)
        own[...] = own[...] + recv[...]
        copies = []
        for d in (1, 3, 2):
            rows = pl.ds(pl.multiple_of(mod4(zl + d) * 64, 64), 64)
            copies.append(send(own.at[rows], zrecv.at[d - 1], dev(dzl=d)))
        return copies

    cs_z = scatter_z(cs_swap, cs_own, cs_recv, zs_recv)
    bt_f3 = forward_y(bt_y3, bt_buf, far, 64)
    arrive(*bt_f0, *bt_f1, *bt_f2, *bt_f3)
    own_at.wait()
    arrive(*at_2)

    def teacher_b(cols):
        return bt_buf[:, :, cols].reshape(2048, 256)

    logits(at_buf, teacher_b, ct_send, 1 - c)
    ct_swap = send(ct_send, ct_recv, dev(dc=1))
    logits(at_buf, teacher_b, ct_own, c)
    ct_z = scatter_z(ct_swap, ct_own, ct_recv, zt_recv)

    mine = pl.ds(pl.multiple_of(zl * 64, 64), 64)

    def scaled(own, zrecv):
        return (own[mine] + zrecv[0] + zrecv[1] + zrecv[2]) * 0.5

    arrive(*cs_z)
    s = scaled(cs_own, zs_recv)
    ms = jnp.max(s, axis=-1, keepdims=True)
    es = jnp.sum(jnp.exp(s - ms), axis=-1, keepdims=True)
    arrive(*ct_z)
    t = scaled(ct_own, zt_recv)
    mt = jnp.max(t, axis=-1, keepdims=True)
    et = jnp.exp(t - mt)
    ws = jnp.sum(et * (t - s), axis=-1, keepdims=True)
    et = jnp.sum(et, axis=-1, keepdims=True)

    lane = lax.broadcasted_iota(jnp.int32, (64, 128), 1)
    stat = jnp.zeros((64, 128), F32)
    for i, col in enumerate((mt, et, ms, es, ws)):
        stat = jnp.where(lane == i, col, stat)
    stat_buf[x] = stat
    stats = [send(stat_buf.at[x], stat_buf.at[x], dev(dx=d)) for d in (1, 3, 2)]

    arrive(*rests)
    rests8 = rest_buf[c * 2 + lax.div(zl, 2)]
    token = lax.broadcasted_iota(jnp.int32, (64, 128), 0) + lax.rem(zl, 2) * 64
    hit = token == lane
    rest_t = jnp.sum(jnp.where(hit, rests8[0:1], 0.0), axis=-1, keepdims=True)
    rest_s = jnp.sum(jnp.where(hit, rests8[1:2], 0.0), axis=-1, keepdims=True)

    arrive(*stats)
    got = [stat_buf[i] for i in range(4)]

    def log_add(a, b):
        top = jnp.maximum(a, b)
        return top + jnp.log(jnp.exp(a - top) + jnp.exp(b - top))

    def whole(k):
        tops = [v[:, k : k + 1] for v in got]
        sums = [v[:, k + 1 : k + 2] for v in got]
        top = jnp.maximum(jnp.maximum(tops[0], tops[1]), jnp.maximum(tops[2], tops[3]))
        scale = [jnp.exp(m - top) for m in tops]
        total = sum(a * b for a, b in zip(sums, scale))
        return top, scale, total

    top_t, scale_t, sum_t = whole(0)
    top_s, _, sum_s = whole(2)
    norm_t = log_add(top_t + jnp.log(sum_t), rest_t)
    norm_s = log_add(top_s + jnp.log(sum_s), rest_s)
    grad = (8.0 * (jnp.exp(s - norm_s) - jnp.exp(t - norm_t))).astype(BF16)
    j = c * 4 + zl
    g_buf[j] = grad
    g_chip = send(g_buf.at[j], g_buf.at[j], dev(dc=1))
    g_z = [send(g_buf.at[j], g_buf.at[j], dev(dzl=d)) for d in (1, 3, 2)]

    weighted = sum(v[:, 4:5] * b for v, b in zip(got, scale_t))
    inside = jnp.exp(top_t - norm_t)
    kl = 16.0 * (weighted * inside - sum_t * inside * (norm_t - norm_s))
    kl_row = jnp.sum(jnp.where(hit, kl, 0.0), axis=0, keepdims=True)
    kl_buf[j] = jnp.broadcast_to(kl_row, (8, 128))
    kls = [
        send(kl_buf.at[j], kl_buf.at[j], dev(dzl=a, dc=b))
        for a in range(4)
        for b in range(2)
        if a + b > 0
    ]

    g_f = []
    for copy, d in zip(g_z, (1, 3, 2)):
        arrive(copy)
        k = c * 4 + mod4(zl - d)
        g_f.append(send(g_buf.at[k], g_buf.at[k], dev(dc=1)))
    arrive(g_chip, *g_f)

    g = g_buf[...].reshape(512, 512)

    def head(i, carry):
        rows = pl.ds(pl.multiple_of(i * 128, 128), 128)
        part = jnp.dot(as_t[rows], g, preferred_element_type=F32)
        gw_send[i] = part.astype(BF16)

        @pl.when(i == y)
        def _():
            gw_own[...] = part

        return carry

    lax.fori_loop(0, 4, head, 0)
    gw_c = [
        send(gw_send.at[mod4(y + d)], gw_recv.at[d - 1], dev(dy=d)) for d in (1, 3, 2)
    ]

    def hidden(i, carry):
        rows = g_buf[pl.ds(i * 2, 2)].reshape(128, 512)
        part = lax.dot_general(
            rows, bs_full[...], (((1,), (1,)), ((), ())), preferred_element_type=F32
        )
        gh_send[i] = part.astype(BF16)

        @pl.when(i == x)
        def _():
            gh_own[...] = part

        return carry

    lax.fori_loop(0, 4, hidden, 0)
    gh_c = [
        send(gh_send.at[mod4(x + d)], gh_recv.at[d - 1], dev(dx=d)) for d in (1, 3, 2)
    ]

    arrive(*gw_c)
    for i in range(16):
        rows = slice(i * 8, (i + 1) * 8)
        part = gw_own[rows]
        for k in range(3):
            wide = gw_recv[k, (i // 2) * 16 : (i // 2) * 16 + 16].astype(F32)
            part = part + wide[(i % 2) * 8 : (i % 2) * 8 + 8]
        w2_send[i] = jnp.concatenate([part[:, :256], part[:, 256:]], axis=0).astype(BF16)
    me = zh * 4 + x
    w2_recv[me] = w2_send[me]
    w2_c = [
        send(w2_send.at[mod4(zh + a) * 4 + mod4(x + b)], w2_recv.at[me], dev(dzh=a, dx=b))
        for a in (2, 1, 3, 0)
        for b in range(4)
        if a + b > 0
    ]

    arrive(*gh_c)
    gh_out[...] = gh_own[...] + sum(gh_recv[k].astype(F32) for k in range(3))
    arrive(*kls)
    k0 = lax.div(x, 2) * 4 + lax.rem(x, 2) * 2
    kl_out[...] = kl_buf[k0, 0:1] + kl_buf[k0 + 1, 0:1]

    arrive(*w2_c)
    for q in range(4):
        both = sum(w2_recv[a * 4 + q].astype(F32) for a in range(4))
        gw_out[:, q * 512 : q * 512 + 256] = both[:8]
        gw_out[:, q * 512 + 256 : (q + 1) * 512] = both[8:]
    for copy in started:
        copy.wait_send()


def body(teacher_hidden, teacher_head, student_hidden, student_head, teacher_rest, student_rest):
    vmem = pl.BlockSpec(memory_space=pltpu.VMEM)
    anywhere = pl.BlockSpec(memory_space=pl.ANY)
    kl, grad_head, grad_hidden = pl.pallas_call(
        distill_kernel,
        out_shape=(
            jax.ShapeDtypeStruct((1, 128), F32),
            jax.ShapeDtypeStruct((8, 2048), F32),
            jax.ShapeDtypeStruct((128, 512), F32),
        ),
        in_specs=[anywhere, anywhere, anywhere, vmem, vmem, vmem],
        out_specs=(vmem, vmem, vmem),
        scratch_shapes=[
            pltpu.VMEM((4, 16, 256), BF16),
            pltpu.VMEM((8, 128), F32),
            pltpu.VMEM((4, 128, 2048), BF16),
            pltpu.VMEM((4, 128, 512), BF16),
            pltpu.VMEM((16, 128, 512), BF16),
            pltpu.VMEM((16, 64, 256), BF16),
            pltpu.VMEM((512, 512), BF16),
            pltpu.VMEM((512, 512), BF16),
            pltpu.VMEM((4, 8, 128), F32),
            pltpu.VMEM((256, 512), F32),
            pltpu.VMEM((256, 512), F32),
            pltpu.VMEM((256, 512), F32),
            pltpu.VMEM((256, 512), F32),
            pltpu.VMEM((256, 512), F32),
            pltpu.VMEM((256, 512), F32),
            pltpu.VMEM((3, 64, 512), F32),
            pltpu.VMEM((3, 64, 512), F32),
            pltpu.VMEM((4, 64, 128), F32),
            pltpu.VMEM((8, 64, 512), BF16),
            pltpu.VMEM((8, 8, 128), F32),
            pltpu.VMEM((128, 512), F32),
            pltpu.VMEM((4, 128, 512), BF16),
            pltpu.VMEM((3, 128, 512), BF16),
            pltpu.VMEM((128, 512), F32),
            pltpu.VMEM((4, 128, 512), BF16),
            pltpu.VMEM((3, 128, 512), BF16),
            pltpu.VMEM((16, 16, 256), BF16),
            pltpu.VMEM((16, 16, 256), BF16),
            pltpu.SemaphoreType.DMA((N_COPY,)),
            pltpu.SemaphoreType.DMA((N_COPY,)),
            pltpu.SemaphoreType.DMA((3,)),
        ],
        compiler_params=pltpu.CompilerParams(
            collective_id=0, has_side_effects=True, vmem_limit_bytes=40 * 1024 * 1024
        ),
    )(
        teacher_hidden,
        teacher_head,
        student_hidden,
        student_head,
        teacher_rest.reshape(1, 128),
        student_rest.reshape(1, 128),
    )
    return kl.reshape(128), grad_head, grad_hidden


def solution(mesh):
    return jax.shard_map(
        body,
        mesh=mesh,
        in_specs=(
            P("fsdp", "role"),
            P(("role", "fsdp"), None),
            P("fsdp", "role"),
            P(("role", "fsdp"), None),
            P("fsdp"),
            P("fsdp"),
        ),
        out_specs=(P("fsdp"), P(("role", "fsdp"), None), P("fsdp", "role")),
        check_vma=False,
    )
```

```python
import jax
import jax.numpy as jnp
from jax import lax
from jax.experimental import pallas as pl
from jax.experimental.pallas import tpu as pltpu
from jax.sharding import PartitionSpec as P

MESH = pl.DeviceIdType.MESH
F32 = jnp.float32
BF16 = jnp.bfloat16
N_COPY = 144


def mod4(v):
    return lax.rem(v + 8, 4)


def distill_kernel(
    at_hbm,
    bt_hbm,
    as_hbm,
    sh_hbm,
    tr_hbm,
    sr_hbm,
    kl_out,
    gw_out,
    gh_out,
    sh_ref,
    tr_ref,
    sr_ref,
    bs_src,
    rest_src,
    at_buf,
    as_buf,
    bt_buf,
    bs_buf,
    bs_full,
    as_t,
    rest_buf,
    ct_send,
    ct_recv,
    ct_own,
    cs_send,
    cs_recv,
    cs_own,
    zt_recv,
    zs_recv,
    stat_buf,
    g_buf,
    kl_buf,
    gh_own,
    gh_send,
    gh_recv,
    gw_own,
    gw_send,
    gw_recv,
    w2_send,
    w2_recv,
    send_sem,
    recv_sem,
    local_sem,
):
    role = lax.axis_index("role")
    fsdp = lax.axis_index("fsdp")
    zl, c = lax.div(role, 2), lax.rem(role, 2)
    zh, y, x = lax.div(fsdp, 16), lax.rem(lax.div(fsdp, 4), 4), lax.rem(fsdp, 4)

    def dev(dzl=0, dc=0, dzh=0, dy=0, dx=0):
        r = mod4(zl + dzl) * 2 + lax.rem(c + dc, 2)
        f = (mod4(zh + dzh) * 4 + mod4(y + dy)) * 4 + mod4(x + dx)
        return (r, f)

    started = []

    def send(src, dst, to):
        k = len(started)
        copy = pltpu.make_async_remote_copy(
            src_ref=src,
            dst_ref=dst,
            send_sem=send_sem.at[k],
            recv_sem=recv_sem.at[k],
            device_id=to,
            device_id_type=MESH,
        )
        copy.start()
        started.append(copy)
        return copy

    def arrive(*copies):
        for copy in copies:
            copy.wait_recv()

    partners = [dev(dzh=a, dx=b) for a in range(4) for b in range(4) if a + b > 0]
    partners += [dev(dy=d) for d in (1, 2, 3)]
    partners += [dev(dzl=a, dc=b) for a in range(4) for b in range(2) if a + b > 0]
    barrier = pltpu.get_barrier_semaphore()
    for to in partners:
        pl.semaphore_signal(barrier, inc=1, device_id=to, device_id_type=MESH)

    own_at = pltpu.make_async_copy(at_hbm, at_buf.at[x], local_sem.at[0])
    own_as = pltpu.make_async_copy(as_hbm, as_buf.at[x], local_sem.at[1])
    piece = zh * 4 + y
    row32 = pl.multiple_of(x * 32, 32)
    row16 = pl.multiple_of(x * 16, 16)
    own_bt = pltpu.make_async_copy(
        bt_hbm.at[:, pl.ds(pl.multiple_of(x * 512, 512), 512)],
        bt_buf.at[piece, pl.ds(row32, 32)],
        local_sem.at[2],
    )
    small = [
        pltpu.make_async_copy(src, dst, local_sem.at[3 + i])
        for i, (src, dst) in enumerate(
            ((sh_hbm, sh_ref), (tr_hbm, tr_ref), (sr_hbm, sr_ref))
        )
    ]
    for copy in small:
        copy.start()
    own_bt.start()
    own_as.start()
    own_at.start()
    for copy in small:
        copy.wait()

    for q in range(4):
        wide = sh_ref[:, q * 512 : (q + 1) * 512].astype(F32)
        bs_src[q] = jnp.concatenate([wide[:, :256], wide[:, 256:]], axis=0).astype(BF16)
    bs_buf[piece, pl.ds(row16, 16)] = bs_src[x]
    r8 = lax.broadcasted_iota(jnp.int32, (8, 128), 0)
    rest = jnp.where(r8 == 0, tr_ref[...], jnp.where(r8 == 1, sr_ref[...], 0.0))
    rest_src[...] = rest
    rest_buf[x] = rest

    pl.semaphore_wait(barrier, len(partners))

    bs_a2a, bt_a2a = [], []
    for d in (1, 3, 2):
        q = mod4(x + d)
        bs_a2a.append(send(bs_src.at[q], bs_buf.at[piece, pl.ds(row16, 16)], dev(dx=d)))
    for d in (1, 3, 2):
        q = mod4(x + d)
        bt_a2a.append(
            send(
                bt_hbm.at[:, pl.ds(pl.multiple_of(q * 512, 512), 512)],
                bt_buf.at[piece, pl.ds(row32, 32)],
                dev(dx=d),
            )
        )
    rests = [send(rest_src, rest_buf.at[x], dev(dx=d)) for d in (1, 3, 2)]

    order = ((1, 0), (3, 1), (1, 1), (3, 0))

    def unit(buf, i, h, rows):
        return buf.at[i, pl.ds(h * rows, rows)]

    def pass_on(buf, i, h, rows, to):
        ref = unit(buf, i, h, rows)
        return send(ref, ref, to)

    def x_start(src, buf):
        return {
            (d, h): send(src.at[pl.ds(h * 64, 64)], unit(buf, x, h, 64), dev(dx=d))
            for d, h in order
        }

    def x_forward(sent, buf):
        arrive(sent[1, 0])
        a = pass_on(buf, mod4(x - 1), 0, 64, dev(dx=1))
        arrive(sent[3, 1])
        b = pass_on(buf, mod4(x + 1), 1, 64, dev(dx=3))
        return [sent[1, 1], sent[3, 0], a, b]

    class Head:
        def __init__(self, buf, rows):
            self.buf, self.rows = buf, rows
            self.zs, self.ys, self.last = {}, {}, []

        def z_start(self, which):
            for d, h in which:
                self.zs[d, h] = pass_on(self.buf, piece, h, self.rows, dev(dzh=d))

        def z_forward(self):
            arrive(self.zs[1, 0])
            a = pass_on(self.buf, prev * 4 + y, 0, self.rows, dev(dzh=1))
            arrive(self.zs[3, 1])
            b = pass_on(self.buf, nxt * 4 + y, 1, self.rows, dev(dzh=3))
            self.zf = (a, b)

        def y_start(self, name, zi, h):
            for d in (1, 3):
                self.ys[name, h, d] = pass_on(
                    self.buf, zi * 4 + y, h, self.rows, dev(dy=d)
                )

        def y_forward(self, name, zi, h):
            d = 1 if h == 0 else 3
            arrive(self.ys[name, h, d])
            i = zi * 4 + mod4(y - 1 if h == 0 else y + 1)
            self.last.append(pass_on(self.buf, i, h, self.rows, dev(dy=d)))
            self.last.append(self.ys[name, h, 4 - d])

    prev, nxt, far = mod4(zh - 1), mod4(zh + 1), mod4(zh + 2)
    st, te = Head(bs_buf, 32), Head(bt_buf, 64)

    as_1 = x_start(as_hbm, as_buf)
    at_1 = x_start(at_hbm, at_buf)

    arrive(*bs_a2a)
    st.z_start(order)
    st.y_start("own", zh, 0)
    st.y_start("own", zh, 1)
    own_bt.wait()
    arrive(*bt_a2a)
    te.z_start(order[:2])
    te.y_start("own", zh, 0)
    te.y_start("own", zh, 1)

    st.z_forward()
    te.z_start(order[2:])
    st.y_start("prev", prev, 0)
    st.y_start("next", nxt, 1)
    st.y_forward("own", zh, 0)
    st.y_forward("own", zh, 1)
    as_2 = x_forward(as_1, as_buf)
    arrive(st.zs[1, 1])
    st.y_start("prev", prev, 1)
    arrive(st.zs[3, 0])
    st.y_start("next", nxt, 0)
    st.y_forward("prev", prev, 0)
    st.y_forward("next", nxt, 1)
    te.y_forward("own", zh, 0)
    te.y_forward("own", zh, 1)
    arrive(st.zf[0])
    st.y_start("far", far, 0)
    arrive(st.zf[1])
    st.y_start("far", far, 1)
    st.y_forward("prev", prev, 1)
    st.y_forward("next", nxt, 0)

    te.z_forward()
    te.y_start("prev", prev, 0)
    te.y_start("next", nxt, 1)
    st.y_forward("far", far, 0)
    st.y_forward("far", far, 1)

    own_as.wait()
    arrive(*as_2)

    def turn(i, carry):
        cols = pl.ds(pl.multiple_of(i * 128, 128), 128)
        block = as_buf[:, :, cols].reshape(512, 128).astype(F32)
        flat = block.T.astype(BF16)
        for yy in range(4):
            at = pl.multiple_of((yy * 4 + i) * 32, 32)
            as_t[pl.ds(at, 32)] = flat[yy * 32 : (yy + 1) * 32]
        return carry

    lax.fori_loop(0, 4, turn, 0)

    arrive(*st.last)
    for i in range(16):
        tall = bs_buf[i].astype(F32).reshape(4, 2, 8, 256)
        rows = slice(i * 32, (i + 1) * 32)
        bs_full[rows, :256] = tall[:, 0].reshape(32, 256).astype(BF16)
        bs_full[rows, 256:] = tall[:, 1].reshape(32, 256).astype(BF16)

    def logits(a_buf, b_of, out, slot):
        a = a_buf[slot]

        def column(i, carry):
            cols = pl.ds(pl.multiple_of(i * 256, 256), 256)
            out[:, cols] = jnp.dot(a, b_of(cols), preferred_element_type=F32)
            return carry

        lax.fori_loop(0, 2, column, 0)

    def both_cores(a_buf, b_of, out_send, out_recv, out_own):
        swaps = []
        for k in range(2):
            logits(a_buf, b_of, out_send.at[k], (1 - c) * 2 + k)
            swaps.append(send(out_send.at[k], out_recv.at[k], dev(dc=1)))
        for k in range(2):
            logits(a_buf, b_of, out_own.at[k], c * 2 + k)
        return swaps

    def student_b(cols):
        return bs_full[:, cols]

    cs_swap = both_cores(as_buf, student_b, cs_send, cs_recv, cs_own)

    def tokens_of(ref, chip):
        return ref.at[lax.div(chip, 2), pl.ds(pl.multiple_of(lax.rem(chip, 2) * 64, 64), 64)]

    def scatter_z(swaps, own, recv, zrecv):
        arrive(*swaps)
        copies = []
        for d in (2, 1, 3, 0):
            mine, theirs = tokens_of(own, mod4(zl + d)), tokens_of(recv, mod4(zl + d))
            mine[...] = mine[...] + theirs[...]
            if d > 0:
                copies.append(send(mine, zrecv.at[d - 1], dev(dzl=d)))
        return copies

    te.y_forward("prev", prev, 0)
    te.y_forward("next", nxt, 1)
    at_2 = x_forward(at_1, at_buf)
    arrive(te.zs[1, 1])
    te.y_start("prev", prev, 1)
    arrive(te.zs[3, 0])
    te.y_start("next", nxt, 0)
    arrive(te.zf[0])
    te.y_start("far", far, 0)
    arrive(te.zf[1])
    te.y_start("far", far, 1)
    cs_z = scatter_z(cs_swap, cs_own, cs_recv, zs_recv)
    te.y_forward("prev", prev, 1)
    te.y_forward("next", nxt, 0)
    te.y_forward("far", far, 0)
    te.y_forward("far", far, 1)
    arrive(*te.last)
    own_at.wait()
    arrive(*at_2)

    def teacher_b(cols):
        return bt_buf[:, :, cols].reshape(2048, 256)

    ct_swap = both_cores(at_buf, teacher_b, ct_send, ct_recv, ct_own)
    ct_z = scatter_z(ct_swap, ct_own, ct_recv, zt_recv)

    def scaled(own, zrecv):
        return (tokens_of(own, zl)[...] + zrecv[0] + zrecv[1] + zrecv[2]) * 0.5

    arrive(*cs_z)
    s = scaled(cs_own, zs_recv)
    ms = jnp.max(s, axis=-1, keepdims=True)
    es = jnp.sum(jnp.exp(s - ms), axis=-1, keepdims=True)
    arrive(*ct_z)
    t = scaled(ct_own, zt_recv)
    mt = jnp.max(t, axis=-1, keepdims=True)
    et = jnp.exp(t - mt)
    ws = jnp.sum(et * (t - s), axis=-1, keepdims=True)
    et = jnp.sum(et, axis=-1, keepdims=True)

    lane = lax.broadcasted_iota(jnp.int32, (64, 128), 1)
    stat = jnp.zeros((64, 128), F32)
    for i, col in enumerate((mt, et, ms, es, ws)):
        stat = jnp.where(lane == i, col, stat)
    stat_buf[x] = stat
    stats = [send(stat_buf.at[x], stat_buf.at[x], dev(dx=d)) for d in (1, 3, 2)]

    arrive(*rests)
    rests8 = rest_buf[c * 2 + lax.div(zl, 2)]
    token = lax.broadcasted_iota(jnp.int32, (64, 128), 0) + lax.rem(zl, 2) * 64
    hit = token == lane
    rest_t = jnp.sum(jnp.where(hit, rests8[0:1], 0.0), axis=-1, keepdims=True)
    rest_s = jnp.sum(jnp.where(hit, rests8[1:2], 0.0), axis=-1, keepdims=True)

    arrive(*stats)
    got = [stat_buf[i] for i in range(4)]

    def log_add(a, b):
        top = jnp.maximum(a, b)
        return top + jnp.log(jnp.exp(a - top) + jnp.exp(b - top))

    def whole(k):
        tops = [v[:, k : k + 1] for v in got]
        sums = [v[:, k + 1 : k + 2] for v in got]
        top = jnp.maximum(jnp.maximum(tops[0], tops[1]), jnp.maximum(tops[2], tops[3]))
        scale = [jnp.exp(m - top) for m in tops]
        total = sum(a * b for a, b in zip(sums, scale))
        return top, scale, total

    top_t, scale_t, sum_t = whole(0)
    top_s, _, sum_s = whole(2)
    norm_t = log_add(top_t + jnp.log(sum_t), rest_t)
    norm_s = log_add(top_s + jnp.log(sum_s), rest_s)
    grad = (8.0 * (jnp.exp(s - norm_s) - jnp.exp(t - norm_t))).astype(BF16)
    j = c * 4 + zl
    g_buf[j] = grad
    g_chip = send(g_buf.at[j], g_buf.at[j], dev(dc=1))
    g_z = [send(g_buf.at[j], g_buf.at[j], dev(dzl=d)) for d in (1, 3, 2)]

    weighted = sum(v[:, 4:5] * b for v, b in zip(got, scale_t))
    inside = jnp.exp(top_t - norm_t)
    kl = 16.0 * (weighted * inside - sum_t * inside * (norm_t - norm_s))
    kl_row = jnp.sum(jnp.where(hit, kl, 0.0), axis=0, keepdims=True)
    kl_buf[j] = jnp.broadcast_to(kl_row, (8, 128))
    kls = [
        send(kl_buf.at[j], kl_buf.at[j], dev(dzl=a, dc=b))
        for a in range(4)
        for b in range(2)
        if a + b > 0
    ]

    g_f = []
    for copy, d in zip(g_z, (1, 3, 2)):
        arrive(copy)
        k = c * 4 + mod4(zl - d)
        g_f.append(send(g_buf.at[k], g_buf.at[k], dev(dc=1)))
    arrive(g_chip, *g_f)

    g = g_buf[...].reshape(512, 512)

    def head(i, carry):
        rows = pl.ds(pl.multiple_of(i * 128, 128), 128)
        part = jnp.dot(as_t[rows], g, preferred_element_type=F32)
        gw_send[i] = part.astype(BF16)

        @pl.when(i == y)
        def _():
            gw_own[...] = part

        return carry

    lax.fori_loop(0, 4, head, 0)
    gw_c = [
        send(gw_send.at[mod4(y + d)], gw_recv.at[d - 1], dev(dy=d)) for d in (1, 3, 2)
    ]

    def hidden(i, carry):
        rows = g_buf[pl.ds(i * 2, 2)].reshape(128, 512)
        part = lax.dot_general(
            rows, bs_full[...], (((1,), (1,)), ((), ())), preferred_element_type=F32
        )
        gh_send[i] = part.astype(BF16)

        @pl.when(i == x)
        def _():
            gh_own[...] = part

        return carry

    lax.fori_loop(0, 4, hidden, 0)
    gh_c = [
        send(gh_send.at[mod4(x + d)], gh_recv.at[d - 1], dev(dx=d)) for d in (1, 3, 2)
    ]

    arrive(*gw_c)
    for i in range(16):
        rows = slice(i * 8, (i + 1) * 8)
        part = gw_own[rows]
        for k in range(3):
            wide = gw_recv[k, (i // 2) * 16 : (i // 2) * 16 + 16].astype(F32)
            part = part + wide[(i % 2) * 8 : (i % 2) * 8 + 8]
        w2_send[i] = jnp.concatenate([part[:, :256], part[:, 256:]], axis=0).astype(BF16)
    me = zh * 4 + x
    w2_recv[me] = w2_send[me]
    w2_c = [
        send(w2_send.at[mod4(zh + a) * 4 + mod4(x + b)], w2_recv.at[me], dev(dzh=a, dx=b))
        for a in (2, 1, 3, 0)
        for b in range(4)
        if a + b > 0
    ]

    arrive(*gh_c)
    gh_out[...] = gh_own[...] + sum(gh_recv[k].astype(F32) for k in range(3))
    arrive(*kls)
    k0 = lax.div(x, 2) * 4 + lax.rem(x, 2) * 2
    kl_out[...] = kl_buf[k0, 0:1] + kl_buf[k0 + 1, 0:1]

    arrive(*w2_c)
    for q in range(4):
        both = sum(w2_recv[a * 4 + q].astype(F32) for a in range(4))
        gw_out[:, q * 512 : q * 512 + 256] = both[:8]
        gw_out[:, q * 512 + 256 : (q + 1) * 512] = both[8:]
    for copy in started:
        copy.wait_send()


def body(teacher_hidden, teacher_head, student_hidden, student_head, teacher_rest, student_rest):
    vmem = pl.BlockSpec(memory_space=pltpu.VMEM)
    hbm = pl.BlockSpec(memory_space=pltpu.HBM)
    kl, grad_head, grad_hidden = pl.pallas_call(
        distill_kernel,
        out_shape=(
            jax.ShapeDtypeStruct((1, 128), F32),
            jax.ShapeDtypeStruct((8, 2048), F32),
            jax.ShapeDtypeStruct((128, 512), F32),
        ),
        in_specs=[hbm] * 6,
        out_specs=(vmem, vmem, vmem),
        scratch_shapes=[
            pltpu.VMEM((8, 2048), BF16),
            pltpu.VMEM((1, 128), F32),
            pltpu.VMEM((1, 128), F32),
            pltpu.VMEM((4, 16, 256), BF16),
            pltpu.VMEM((8, 128), F32),
            pltpu.VMEM((4, 128, 2048), BF16),
            pltpu.VMEM((4, 128, 512), BF16),
            pltpu.VMEM((16, 128, 512), BF16),
            pltpu.VMEM((16, 64, 256), BF16),
            pltpu.VMEM((512, 512), BF16),
            pltpu.VMEM((512, 512), BF16),
            pltpu.VMEM((4, 8, 128), F32),
            pltpu.VMEM((2, 128, 512), F32),
            pltpu.VMEM((2, 128, 512), F32),
            pltpu.VMEM((2, 128, 512), F32),
            pltpu.VMEM((2, 128, 512), F32),
            pltpu.VMEM((2, 128, 512), F32),
            pltpu.VMEM((2, 128, 512), F32),
            pltpu.VMEM((3, 64, 512), F32),
            pltpu.VMEM((3, 64, 512), F32),
            pltpu.VMEM((4, 64, 128), F32),
            pltpu.VMEM((8, 64, 512), BF16),
            pltpu.VMEM((8, 8, 128), F32),
            pltpu.VMEM((128, 512), F32),
            pltpu.VMEM((4, 128, 512), BF16),
            pltpu.VMEM((3, 128, 512), BF16),
            pltpu.VMEM((128, 512), F32),
            pltpu.VMEM((4, 128, 512), BF16),
            pltpu.VMEM((3, 128, 512), BF16),
            pltpu.VMEM((16, 16, 256), BF16),
            pltpu.VMEM((16, 16, 256), BF16),
            pltpu.SemaphoreType.DMA((N_COPY,)),
            pltpu.SemaphoreType.DMA((N_COPY,)),
            pltpu.SemaphoreType.DMA((6,)),
        ],
        compiler_params=pltpu.CompilerParams(
            collective_id=0, has_side_effects=True, vmem_limit_bytes=63 * 1024 * 1024
        ),
    )(
        teacher_hidden,
        teacher_head,
        student_hidden,
        student_head,
        teacher_rest.reshape(1, 128),
        student_rest.reshape(1, 128),
    )
    return kl.reshape(128), grad_head, grad_hidden


def solution(mesh):
    return jax.shard_map(
        body,
        mesh=mesh,
        in_specs=(
            P("fsdp", "role"),
            P(("role", "fsdp"), None),
            P("fsdp", "role"),
            P(("role", "fsdp"), None),
            P("fsdp"),
            P("fsdp"),
        ),
        out_specs=(P("fsdp"), P(("role", "fsdp"), None), P("fsdp", "role")),
        check_vma=False,
    )
```

```python
import jax
import jax.numpy as jnp
from jax import lax
from jax.experimental import pallas as pl
from jax.experimental.pallas import tpu as pltpu
from jax.sharding import PartitionSpec as P

MESH = pl.DeviceIdType.MESH
F32 = jnp.float32
BF16 = jnp.bfloat16
N_COPY = 144


def mod4(v):
    return lax.rem(v + 8, 4)


def distill_kernel(
    at_hbm,
    bt_hbm,
    as_hbm,
    sh_hbm,
    tr_hbm,
    sr_hbm,
    kl_out,
    gw_out,
    gh_out,
    sh_ref,
    tr_ref,
    sr_ref,
    bs_src,
    rest_src,
    at_buf,
    as_buf,
    bt_buf,
    bs_buf,
    bs_full,
    as_t,
    rest_buf,
    ct_send,
    ct_recv,
    ct_own,
    cs_send,
    cs_recv,
    cs_own,
    zt_recv,
    zs_recv,
    stat_buf,
    g_buf,
    kl_buf,
    gh_own,
    gh_send,
    gh_recv,
    gw_own,
    gw_send,
    gw_recv,
    w_own,
    w_send,
    w_recv,
    x_send,
    kl_vmem,
    gw_vmem,
    gh_vmem,
    send_sem,
    recv_sem,
    local_sem,
):
    role = lax.axis_index("role")
    fsdp = lax.axis_index("fsdp")
    zl, c = lax.div(role, 2), lax.rem(role, 2)
    zh, y, x = lax.div(fsdp, 16), lax.rem(lax.div(fsdp, 4), 4), lax.rem(fsdp, 4)

    def dev(dzl=0, dc=0, dzh=0, dy=0, dx=0):
        r = mod4(zl + dzl) * 2 + lax.rem(c + dc, 2)
        f = (mod4(zh + dzh) * 4 + mod4(y + dy)) * 4 + mod4(x + dx)
        return (r, f)

    started = []

    def send(src, dst, to):
        k = len(started)
        copy = pltpu.make_async_remote_copy(
            src_ref=src,
            dst_ref=dst,
            send_sem=send_sem.at[k],
            recv_sem=recv_sem.at[k],
            device_id=to,
            device_id_type=MESH,
        )
        copy.start()
        started.append(copy)
        return copy

    def arrive(*copies):
        for copy in copies:
            copy.wait_recv()

    partners = [dev(dzh=d) for d in (1, 2, 3)] + [dev(dx=d) for d in (1, 2, 3)]
    partners += [dev(dy=d) for d in (1, 2, 3)]
    partners += [dev(dzl=a, dc=b) for a in range(4) for b in range(2) if a + b > 0]
    barrier = pltpu.get_barrier_semaphore()
    for to in partners:
        pl.semaphore_signal(barrier, inc=1, device_id=to, device_id_type=MESH)

    own_at = pltpu.make_async_copy(at_hbm, at_buf.at[x], local_sem.at[0])
    own_as = pltpu.make_async_copy(as_hbm, as_buf.at[x], local_sem.at[1])
    piece = zh * 4 + y
    row32 = pl.multiple_of(x * 32, 32)
    row16 = pl.multiple_of(x * 16, 16)
    own_bt = pltpu.make_async_copy(
        bt_hbm.at[:, pl.ds(pl.multiple_of(x * 512, 512), 512)],
        bt_buf.at[piece, pl.ds(row32, 32)],
        local_sem.at[2],
    )
    small = [
        pltpu.make_async_copy(src, dst, local_sem.at[3 + i])
        for i, (src, dst) in enumerate(
            ((sh_hbm, sh_ref), (tr_hbm, tr_ref), (sr_hbm, sr_ref))
        )
    ]
    for copy in small:
        copy.start()
    own_bt.start()
    own_as.start()
    own_at.start()
    for copy in small:
        copy.wait()

    for q in range(4):
        wide = sh_ref[:, q * 512 : (q + 1) * 512].astype(F32)
        bs_src[q] = jnp.concatenate([wide[:, :256], wide[:, 256:]], axis=0).astype(BF16)
    bs_buf[piece, pl.ds(row16, 16)] = bs_src[x]
    r8 = lax.broadcasted_iota(jnp.int32, (8, 128), 0)
    rest = jnp.where(r8 == 0, tr_ref[...], jnp.where(r8 == 1, sr_ref[...], 0.0))
    rest_src[...] = rest
    rest_buf[x] = rest

    pl.semaphore_wait(barrier, len(partners))

    bs_a2a, bt_a2a = [], []
    for d in (1, 3, 2):
        q = mod4(x + d)
        bs_a2a.append(send(bs_src.at[q], bs_buf.at[piece, pl.ds(row16, 16)], dev(dx=d)))
    for d in (1, 3, 2):
        q = mod4(x + d)
        bt_a2a.append(
            send(
                bt_hbm.at[:, pl.ds(pl.multiple_of(q * 512, 512), 512)],
                bt_buf.at[piece, pl.ds(row32, 32)],
                dev(dx=d),
            )
        )
    rests = [send(rest_src, rest_buf.at[x], dev(dx=d)) for d in (1, 3, 2)]

    order = ((1, 0), (3, 1), (1, 1), (3, 0))

    def unit(buf, i, h, rows):
        return buf.at[i, pl.ds(h * rows, rows)]

    def pass_on(buf, i, h, rows, to):
        ref = unit(buf, i, h, rows)
        return send(ref, ref, to)

    def x_start(src, buf):
        return {
            (d, h): send(src.at[pl.ds(h * 64, 64)], unit(buf, x, h, 64), dev(dx=d))
            for d, h in order
        }

    def x_forward(sent, buf):
        arrive(sent[1, 0])
        a = pass_on(buf, mod4(x - 1), 0, 64, dev(dx=1))
        arrive(sent[3, 1])
        b = pass_on(buf, mod4(x + 1), 1, 64, dev(dx=3))
        return [sent[1, 1], sent[3, 0], a, b]

    class Head:
        def __init__(self, buf, rows):
            self.buf, self.rows = buf, rows
            self.zs, self.ys, self.last = {}, {}, []

        def z_start(self, which):
            for d, h in which:
                self.zs[d, h] = pass_on(self.buf, piece, h, self.rows, dev(dzh=d))

        def z_forward(self):
            arrive(self.zs[1, 0])
            a = pass_on(self.buf, prev * 4 + y, 0, self.rows, dev(dzh=1))
            arrive(self.zs[3, 1])
            b = pass_on(self.buf, nxt * 4 + y, 1, self.rows, dev(dzh=3))
            self.zf = (a, b)

        def y_start(self, name, zi, h):
            for d in (1, 3):
                self.ys[name, h, d] = pass_on(
                    self.buf, zi * 4 + y, h, self.rows, dev(dy=d)
                )

        def y_forward(self, name, zi, h):
            d = 1 if h == 0 else 3
            arrive(self.ys[name, h, d])
            i = zi * 4 + mod4(y - 1 if h == 0 else y + 1)
            self.last.append(pass_on(self.buf, i, h, self.rows, dev(dy=d)))
            self.last.append(self.ys[name, h, 4 - d])

    prev, nxt, far = mod4(zh - 1), mod4(zh + 1), mod4(zh + 2)
    st, te = Head(bs_buf, 32), Head(bt_buf, 64)

    as_1 = x_start(as_hbm, as_buf)
    at_1 = x_start(at_hbm, at_buf)

    arrive(*bs_a2a)
    st.z_start(order)
    st.y_start("own", zh, 0)
    st.y_start("own", zh, 1)
    own_bt.wait()
    arrive(*bt_a2a)
    te.z_start(order[:2])
    te.y_start("own", zh, 0)
    te.y_start("own", zh, 1)

    st.z_forward()
    te.z_start(order[2:])
    st.y_start("prev", prev, 0)
    st.y_start("next", nxt, 1)
    st.y_forward("own", zh, 0)
    st.y_forward("own", zh, 1)
    as_2 = x_forward(as_1, as_buf)
    arrive(st.zs[1, 1])
    st.y_start("prev", prev, 1)
    arrive(st.zs[3, 0])
    st.y_start("next", nxt, 0)
    st.y_forward("prev", prev, 0)
    st.y_forward("next", nxt, 1)
    te.y_forward("own", zh, 0)
    te.y_forward("own", zh, 1)
    arrive(st.zf[0])
    st.y_start("far", far, 0)
    arrive(st.zf[1])
    st.y_start("far", far, 1)
    st.y_forward("prev", prev, 1)
    st.y_forward("next", nxt, 0)

    te.z_forward()
    te.y_start("prev", prev, 0)
    te.y_start("next", nxt, 1)
    st.y_forward("far", far, 0)
    st.y_forward("far", far, 1)

    own_as.wait()
    arrive(*as_2)

    def turn(i, carry):
        cols = pl.ds(pl.multiple_of(i * 128, 128), 128)
        block = as_buf[:, :, cols].reshape(512, 128).astype(F32)
        flat = block.T.astype(BF16)
        for yy in range(4):
            at = pl.multiple_of((yy * 4 + i) * 32, 32)
            as_t[pl.ds(at, 32)] = flat[yy * 32 : (yy + 1) * 32]
        return carry

    lax.fori_loop(0, 4, turn, 0)

    arrive(*st.last)
    for i in range(16):
        tall = bs_buf[i].astype(F32).reshape(4, 2, 8, 256)
        rows = slice(i * 32, (i + 1) * 32)
        bs_full[rows, :256] = tall[:, 0].reshape(32, 256).astype(BF16)
        bs_full[rows, 256:] = tall[:, 1].reshape(32, 256).astype(BF16)

    def logits(a_buf, b_of, out, slot):
        a = a_buf[slot]

        def column(i, carry):
            cols = pl.ds(pl.multiple_of(i * 256, 256), 256)
            out[:, cols] = jnp.dot(a, b_of(cols), preferred_element_type=F32)
            return carry

        lax.fori_loop(0, 2, column, 0)

    def both_cores(a_buf, b_of, out_send, out_recv, out_own):
        swaps = []
        for k in range(2):
            logits(a_buf, b_of, out_send.at[k], (1 - c) * 2 + k)
            swaps.append(send(out_send.at[k], out_recv.at[k], dev(dc=1)))
        for k in range(2):
            logits(a_buf, b_of, out_own.at[k], c * 2 + k)
        return swaps

    def student_b(cols):
        return bs_full[:, cols]

    cs_swap = both_cores(as_buf, student_b, cs_send, cs_recv, cs_own)

    def tokens_of(ref, chip):
        return ref.at[lax.div(chip, 2), pl.ds(pl.multiple_of(lax.rem(chip, 2) * 64, 64), 64)]

    def scatter_z(swaps, own, recv, zrecv):
        arrive(*swaps)
        copies = []
        for d in (2, 1, 3, 0):
            mine, theirs = tokens_of(own, mod4(zl + d)), tokens_of(recv, mod4(zl + d))
            mine[...] = mine[...] + theirs[...]
            if d > 0:
                copies.append(send(mine, zrecv.at[d - 1], dev(dzl=d)))
        return copies

    te.y_forward("prev", prev, 0)
    te.y_forward("next", nxt, 1)
    at_2 = x_forward(at_1, at_buf)
    arrive(te.zs[1, 1])
    te.y_start("prev", prev, 1)
    arrive(te.zs[3, 0])
    te.y_start("next", nxt, 0)
    arrive(te.zf[0])
    te.y_start("far", far, 0)
    arrive(te.zf[1])
    te.y_start("far", far, 1)
    cs_z = scatter_z(cs_swap, cs_own, cs_recv, zs_recv)
    te.y_forward("prev", prev, 1)
    te.y_forward("next", nxt, 0)
    te.y_forward("far", far, 0)
    te.y_forward("far", far, 1)
    arrive(*te.last)
    own_at.wait()
    arrive(*at_2)

    def teacher_b(cols):
        return bt_buf[:, :, cols].reshape(2048, 256)

    ct_swap = both_cores(at_buf, teacher_b, ct_send, ct_recv, ct_own)
    ct_z = scatter_z(ct_swap, ct_own, ct_recv, zt_recv)

    def scaled(own, zrecv):
        return (tokens_of(own, zl)[...] + zrecv[0] + zrecv[1] + zrecv[2]) * 0.5

    arrive(*cs_z)
    s = scaled(cs_own, zs_recv)
    ms = jnp.max(s, axis=-1, keepdims=True)
    es = jnp.sum(jnp.exp(s - ms), axis=-1, keepdims=True)
    arrive(*ct_z)
    t = scaled(ct_own, zt_recv)
    mt = jnp.max(t, axis=-1, keepdims=True)
    et = jnp.exp(t - mt)
    ws = jnp.sum(et * (t - s), axis=-1, keepdims=True)
    et = jnp.sum(et, axis=-1, keepdims=True)

    lane = lax.broadcasted_iota(jnp.int32, (64, 128), 1)
    stat = jnp.zeros((64, 128), F32)
    for i, col in enumerate((mt, et, ms, es, ws)):
        stat = jnp.where(lane == i, col, stat)
    flat = stat.T[:8]
    stat_buf[x] = jnp.concatenate([flat, flat], axis=1)
    stats = [send(stat_buf.at[x], stat_buf.at[x], dev(dx=d)) for d in (1, 3, 2)]
    arrive(*rests)
    arrive(*stats)
    got = [stat_buf[i] for i in range(4)]
    rests8 = rest_buf[c * 2 + lax.div(zl, 2)]

    def log_add(a, b):
        top = jnp.maximum(a, b)
        return top + jnp.log(jnp.exp(a - top) + jnp.exp(b - top))

    def whole(k):
        tops = [v[k : k + 1] for v in got]
        sums = [v[k + 1 : k + 2] for v in got]
        top = jnp.maximum(jnp.maximum(tops[0], tops[1]), jnp.maximum(tops[2], tops[3]))
        scale = [jnp.exp(m - top) for m in tops]
        total = sum(a * b for a, b in zip(sums, scale))
        return top, scale, total

    top_t, scale_t, sum_t = whole(0)
    top_s, _, sum_s = whole(2)
    norm_t = log_add(top_t + jnp.log(sum_t), rests8[0:1])
    norm_s = log_add(top_s + jnp.log(sum_s), rests8[1:2])
    upper = lax.rem(zl, 2)
    square = lax.broadcasted_iota(jnp.int32, (128, 128), 0)
    turned = jnp.where(square == 0, norm_t, norm_s).T
    turned = jnp.where(upper == 0, turned[:64], turned[64:])
    col_t, col_s = turned[:, 0:1], turned[:, 1:2]

    j = c * 4 + zl
    g_z, g_chip = [], []
    for v in range(2):
        cols = slice(v * 256, (v + 1) * 256)
        gap = jnp.exp(s[:, cols] - col_s) - jnp.exp(t[:, cols] - col_t)
        g_buf[v, j] = (8.0 * gap).astype(BF16)
        mine = g_buf.at[v, j]
        g_z.append([send(mine, mine, dev(dzl=d)) for d in (2, 1, 3)])
        g_chip.append(send(mine, mine, dev(dc=1)))

    weighted = sum(v[4:5] * b for v, b in zip(got, scale_t))
    inside = jnp.exp(top_t - norm_t)
    kl = 16.0 * (weighted * inside - sum_t * inside * (norm_t - norm_s))
    half_of = lax.div(lax.broadcasted_iota(jnp.int32, (1, 128), 1), 64)
    kl_buf[j] = jnp.broadcast_to(jnp.where(half_of == upper, kl, 0.0), (8, 128))
    kls = [
        send(kl_buf.at[j], kl_buf.at[j], dev(dzl=a, dc=b))
        for a in range(4)
        for b in range(2)
        if a + b > 0
    ]

    gw_c, gh_c = [], []
    for v in range(2):
        g_f = []
        for copy, d in zip(g_z[v], (2, 1, 3)):
            arrive(copy)
            theirs = g_buf.at[v, c * 4 + mod4(zl - d)]
            g_f.append(send(theirs, theirs, dev(dc=1)))
        arrive(g_chip[v], *g_f)

        g = g_buf[v].reshape(512, 256)
        sent = []
        for d in (2, 1, 3, 0):
            rows = pl.ds(pl.multiple_of(mod4(y + d) * 128, 128), 128)
            part = jnp.dot(as_t[rows], g, preferred_element_type=F32)
            if d == 0:
                gw_own[v] = part
            else:
                gw_send[v, d - 1] = part.astype(BF16)
                sent.append(send(gw_send.at[v, d - 1], gw_recv.at[v, d - 1], dev(dy=d)))
        gw_c.append(sent)

        for d in (2, 1, 3, 0):
            rows = g_buf[v, pl.ds(mod4(x + d) * 2, 2)].reshape(128, 256)
            part = lax.dot_general(
                rows,
                bs_full[:, v * 256 : (v + 1) * 256],
                (((1,), (1,)), ((), ())),
                preferred_element_type=F32,
            )
            if v == 0:
                gh_own[d] = part
            elif d == 0:
                gh_own[0] = gh_own[0] + part
            else:
                gh_send[d - 1] = (gh_own[d] + part).astype(BF16)
                gh_c.append(send(gh_send.at[d - 1], gh_recv.at[d - 1], dev(dx=d)))

    w_c = []
    for v in range(2):
        arrive(*gw_c[v])
        total = gw_own[v] + sum(gw_recv[v, k].astype(F32) for k in range(3))
        total = total.reshape(4, 32, 256)
        w_own[v] = total
        w_send[v] = total.astype(BF16)
        w_c.append(
            [
                send(w_send.at[v, mod4(zh + d)], w_recv.at[v, d - 1], dev(dzh=d))
                for d in (2, 1, 3)
            ]
        )

    def write_out(src, dst, k):
        copy = pltpu.make_async_copy(src, dst, local_sem.at[k])
        copy.start()
        return copy

    arrive(*gh_c)
    gh_vmem[...] = gh_own[0] + sum(gh_recv[k].astype(F32) for k in range(3))
    outs = [write_out(gh_vmem, gh_out, 6)]
    arrive(*kls)
    k0 = lax.div(x, 2) * 4 + lax.rem(x, 2) * 2
    kl_vmem[...] = kl_buf[k0, 0:1] + kl_buf[k0 + 1, 0:1]
    outs.append(write_out(kl_vmem, kl_out, 7))

    x_c = []
    for v in range(2):
        arrive(*w_c[v])
        rows = w_own[v, zh] + sum(w_recv[v, k].astype(F32) for k in range(3))
        x_send[v] = rows.reshape(4, 8, 256)
        cols = pl.ds(pl.multiple_of(x * 512 + v * 256, 256), 256)
        gw_vmem[:, cols] = x_send[v, x]
        x_c += [
            send(x_send.at[v, mod4(x + d)], gw_vmem.at[:, cols], dev(dx=d))
            for d in (2, 1, 3)
        ]
    for copy in started:
        copy.wait_send()
    arrive(*x_c)
    outs.append(write_out(gw_vmem, gw_out, 8))
    for copy in outs:
        copy.wait()


def settle_kernel(kl_in, gw_in, gh_in, kl_out, gw_out, gh_out, kl_vmem, gw_vmem, gh_vmem, sem):
    ways = ((gh_in, gh_vmem, gh_out), (gw_in, gw_vmem, gw_out), (kl_in, kl_vmem, kl_out))
    into = [pltpu.make_async_copy(a, b, sem.at[i]) for i, (a, b, _) in enumerate(ways)]
    onto = [pltpu.make_async_copy(b, o, sem.at[3 + i]) for i, (_, b, o) in enumerate(ways)]
    for copy in into:
        copy.start()
    for first, then in zip(into, onto):
        first.wait()
        then.start()
    for copy in onto:
        copy.wait()


def body(teacher_hidden, teacher_head, student_hidden, student_head, teacher_rest, student_rest):
    hbm = pl.BlockSpec(memory_space=pltpu.HBM)
    out_shape = (
        jax.ShapeDtypeStruct((1, 128), F32),
        jax.ShapeDtypeStruct((8, 2048), F32),
        jax.ShapeDtypeStruct((128, 512), F32),
    )
    results = pl.pallas_call(
        distill_kernel,
        out_shape=out_shape,
        in_specs=[hbm] * 6,
        out_specs=(hbm, hbm, hbm),
        scratch_shapes=[
            pltpu.VMEM((8, 2048), BF16),
            pltpu.VMEM((1, 128), F32),
            pltpu.VMEM((1, 128), F32),
            pltpu.VMEM((4, 16, 256), BF16),
            pltpu.VMEM((8, 128), F32),
            pltpu.VMEM((4, 128, 2048), BF16),
            pltpu.VMEM((4, 128, 512), BF16),
            pltpu.VMEM((16, 128, 512), BF16),
            pltpu.VMEM((16, 64, 256), BF16),
            pltpu.VMEM((512, 512), BF16),
            pltpu.VMEM((512, 512), BF16),
            pltpu.VMEM((4, 8, 128), F32),
            pltpu.VMEM((2, 128, 512), F32),
            pltpu.VMEM((2, 128, 512), F32),
            pltpu.VMEM((2, 128, 512), F32),
            pltpu.VMEM((2, 128, 512), F32),
            pltpu.VMEM((2, 128, 512), F32),
            pltpu.VMEM((2, 128, 512), F32),
            pltpu.VMEM((3, 64, 512), F32),
            pltpu.VMEM((3, 64, 512), F32),
            pltpu.VMEM((4, 8, 128), F32),
            pltpu.VMEM((2, 8, 64, 256), BF16),
            pltpu.VMEM((8, 8, 128), F32),
            pltpu.VMEM((4, 128, 512), F32),
            pltpu.VMEM((3, 128, 512), BF16),
            pltpu.VMEM((3, 128, 512), BF16),
            pltpu.VMEM((2, 128, 256), F32),
            pltpu.VMEM((2, 3, 128, 256), BF16),
            pltpu.VMEM((2, 3, 128, 256), BF16),
            pltpu.VMEM((2, 4, 32, 256), F32),
            pltpu.VMEM((2, 4, 32, 256), BF16),
            pltpu.VMEM((2, 3, 32, 256), BF16),
            pltpu.VMEM((2, 4, 8, 256), F32),
            pltpu.VMEM((1, 128), F32),
            pltpu.VMEM((8, 2048), F32),
            pltpu.VMEM((128, 512), F32),
            pltpu.SemaphoreType.DMA((N_COPY,)),
            pltpu.SemaphoreType.DMA((N_COPY,)),
            pltpu.SemaphoreType.DMA((9,)),
        ],
        compiler_params=pltpu.CompilerParams(
            collective_id=0, has_side_effects=True, vmem_limit_bytes=63 * 1024 * 1024
        ),
    )(
        teacher_hidden,
        teacher_head,
        student_hidden,
        student_head,
        teacher_rest.reshape(1, 128),
        student_rest.reshape(1, 128),
    )
    kl, grad_head, grad_hidden = pl.pallas_call(
        settle_kernel,
        out_shape=out_shape,
        in_specs=[hbm] * 3,
        out_specs=(hbm, hbm, hbm),
        scratch_shapes=[
            pltpu.VMEM((1, 128), F32),
            pltpu.VMEM((8, 2048), F32),
            pltpu.VMEM((128, 512), F32),
            pltpu.SemaphoreType.DMA((6,)),
        ],
        compiler_params=pltpu.CompilerParams(vmem_limit_bytes=63 * 1024 * 1024),
    )(*results)
    return kl.reshape(128), grad_head, grad_hidden


def solution(mesh):
    return jax.shard_map(
        body,
        mesh=mesh,
        in_specs=(
            P("fsdp", "role"),
            P(("role", "fsdp"), None),
            P("fsdp", "role"),
            P(("role", "fsdp"), None),
            P("fsdp"),
            P("fsdp"),
        ),
        out_specs=(P("fsdp"), P(("role", "fsdp"), None), P("fsdp", "role")),
        check_vma=False,
    )
```

```python
import jax
import jax.numpy as jnp
from jax import lax
from jax.experimental import pallas as pl
from jax.experimental.pallas import tpu as pltpu
from jax.sharding import PartitionSpec as P

MESH = pl.DeviceIdType.MESH
F32 = jnp.float32
BF16 = jnp.bfloat16
N_COPY = 144


def mod4(v):
    return lax.rem(v + 8, 4)


def distill_kernel(
    at_hbm,
    bt_hbm,
    as_hbm,
    sh_hbm,
    tr_hbm,
    sr_hbm,
    kl_out,
    gw_out,
    gh_out,
    sh_ref,
    tr_ref,
    sr_ref,
    bs_src,
    rest_src,
    at_buf,
    as_buf,
    bt_buf,
    bs_buf,
    bs_full,
    as_t,
    rest_buf,
    ct_send,
    ct_recv,
    ct_own,
    cs_send,
    cs_recv,
    cs_own,
    zt_send,
    zs_send,
    zt_recv,
    zs_recv,
    stat_buf,
    g_buf,
    kl_buf,
    gh_own,
    gh_send,
    gh_recv,
    gw_own,
    gw_send,
    gw_recv,
    w_own,
    w_send,
    w_recv,
    x_send,
    kl_vmem,
    gw_vmem,
    gh_vmem,
    send_sem,
    recv_sem,
    local_sem,
):
    role = lax.axis_index("role")
    fsdp = lax.axis_index("fsdp")
    zl, c = lax.div(role, 2), lax.rem(role, 2)
    zh, y, x = lax.div(fsdp, 16), lax.rem(lax.div(fsdp, 4), 4), lax.rem(fsdp, 4)

    def dev(dzl=0, dc=0, dzh=0, dy=0, dx=0):
        r = mod4(zl + dzl) * 2 + lax.rem(c + dc, 2)
        f = (mod4(zh + dzh) * 4 + mod4(y + dy)) * 4 + mod4(x + dx)
        return (r, f)

    started, pending = [], []

    def send(src, dst, to):
        k = len(started)
        copy = pltpu.make_async_remote_copy(
            src_ref=src,
            dst_ref=dst,
            send_sem=send_sem.at[k],
            recv_sem=recv_sem.at[k],
            device_id=to,
            device_id_type=MESH,
        )
        copy.start()
        started.append(copy)
        pending.append(copy)
        return copy

    def drain():
        while pending:
            pending.pop(0).wait_send()

    def arrive(*copies):
        for copy in copies:
            copy.wait_recv()

    partners = [dev(dzh=d) for d in (1, 2, 3)] + [dev(dx=d) for d in (1, 2, 3)]
    partners += [dev(dy=d) for d in (1, 2, 3)]
    partners += [dev(dzl=a, dc=b) for a in range(4) for b in range(2) if a + b > 0]
    barrier = pltpu.get_barrier_semaphore()
    for to in partners:
        pl.semaphore_signal(barrier, inc=1, device_id=to, device_id_type=MESH)

    own_at = pltpu.make_async_copy(at_hbm, at_buf.at[x], local_sem.at[0])
    own_as = pltpu.make_async_copy(as_hbm, as_buf.at[x], local_sem.at[1])
    piece = zh * 4 + y
    row32 = pl.multiple_of(x * 32, 32)
    row16 = pl.multiple_of(x * 16, 16)
    own_bt = pltpu.make_async_copy(
        bt_hbm.at[:, pl.ds(pl.multiple_of(x * 512, 512), 512)],
        bt_buf.at[piece, pl.ds(row32, 32)],
        local_sem.at[2],
    )
    small = [
        pltpu.make_async_copy(src, dst, local_sem.at[3 + i])
        for i, (src, dst) in enumerate(
            ((sh_hbm, sh_ref), (tr_hbm, tr_ref), (sr_hbm, sr_ref))
        )
    ]
    for copy in small:
        copy.start()
    own_bt.start()
    own_as.start()
    own_at.start()
    for copy in small:
        copy.wait()

    for q in range(4):
        wide = sh_ref[:, q * 512 : (q + 1) * 512].astype(F32)
        bs_src[q] = jnp.concatenate([wide[:, :256], wide[:, 256:]], axis=0).astype(BF16)
    bs_buf[piece, pl.ds(row16, 16)] = bs_src[x]
    r8 = lax.broadcasted_iota(jnp.int32, (8, 128), 0)
    rest = jnp.where(r8 == 0, tr_ref[...], jnp.where(r8 == 1, sr_ref[...], 0.0))
    rest_src[...] = rest
    rest_buf[x] = rest

    pl.semaphore_wait(barrier, len(partners))

    bs_a2a, bt_a2a = [], []
    for d in (1, 3, 2):
        q = mod4(x + d)
        bs_a2a.append(send(bs_src.at[q], bs_buf.at[piece, pl.ds(row16, 16)], dev(dx=d)))
    for d in (1, 3, 2):
        q = mod4(x + d)
        bt_a2a.append(
            send(
                bt_hbm.at[:, pl.ds(pl.multiple_of(q * 512, 512), 512)],
                bt_buf.at[piece, pl.ds(row32, 32)],
                dev(dx=d),
            )
        )
    rests = [send(rest_src, rest_buf.at[x], dev(dx=d)) for d in (1, 3, 2)]

    order = ((1, 0), (3, 1), (1, 1), (3, 0))

    def unit(buf, i, h, rows):
        return buf.at[i, pl.ds(h * rows, rows)]

    def pass_on(buf, i, h, rows, to):
        ref = unit(buf, i, h, rows)
        return send(ref, ref, to)

    def x_start(src, buf):
        return {
            (d, h): send(src.at[pl.ds(h * 64, 64)], unit(buf, x, h, 64), dev(dx=d))
            for d, h in order
        }

    def x_forward(sent, buf):
        arrive(sent[1, 0])
        a = pass_on(buf, mod4(x - 1), 0, 64, dev(dx=1))
        arrive(sent[3, 1])
        b = pass_on(buf, mod4(x + 1), 1, 64, dev(dx=3))
        return [sent[1, 1], sent[3, 0], a, b]

    class Head:
        def __init__(self, buf, rows):
            self.buf, self.rows = buf, rows
            self.zs, self.ys, self.last = {}, {}, []

        def z_start(self, which):
            for d, h in which:
                self.zs[d, h] = pass_on(self.buf, piece, h, self.rows, dev(dzh=d))

        def z_forward(self):
            arrive(self.zs[1, 0])
            a = pass_on(self.buf, prev * 4 + y, 0, self.rows, dev(dzh=1))
            arrive(self.zs[3, 1])
            b = pass_on(self.buf, nxt * 4 + y, 1, self.rows, dev(dzh=3))
            self.zf = (a, b)

        def y_start(self, name, zi, h):
            for d in (1, 3):
                self.ys[name, h, d] = pass_on(
                    self.buf, zi * 4 + y, h, self.rows, dev(dy=d)
                )

        def y_forward(self, name, zi, h):
            d = 1 if h == 0 else 3
            arrive(self.ys[name, h, d])
            i = zi * 4 + mod4(y - 1 if h == 0 else y + 1)
            self.last.append(pass_on(self.buf, i, h, self.rows, dev(dy=d)))
            self.last.append(self.ys[name, h, 4 - d])

    prev, nxt, far = mod4(zh - 1), mod4(zh + 1), mod4(zh + 2)
    st, te = Head(bs_buf, 32), Head(bt_buf, 64)

    as_1 = x_start(as_hbm, as_buf)
    at_1 = x_start(at_hbm, at_buf)

    arrive(*bs_a2a)
    st.z_start(order)
    st.y_start("own", zh, 0)
    st.y_start("own", zh, 1)
    own_bt.wait()
    arrive(*bt_a2a)
    te.z_start(order[:2])
    te.y_start("own", zh, 0)
    te.y_start("own", zh, 1)

    st.z_forward()
    te.z_start(order[2:])
    st.y_start("prev", prev, 0)
    st.y_start("next", nxt, 1)
    as_2 = x_forward(as_1, as_buf)
    st.y_forward("own", zh, 0)
    st.y_forward("own", zh, 1)
    arrive(st.zs[1, 1])
    st.y_start("prev", prev, 1)
    arrive(st.zs[3, 0])
    st.y_start("next", nxt, 0)
    st.y_forward("prev", prev, 0)
    st.y_forward("next", nxt, 1)
    te.y_forward("own", zh, 0)
    te.y_forward("own", zh, 1)
    st.y_forward("prev", prev, 1)
    st.y_forward("next", nxt, 0)
    at_2 = x_forward(at_1, at_buf)
    te.z_forward()
    te.y_start("prev", prev, 0)
    te.y_start("next", nxt, 1)
    arrive(st.zf[0])
    st.y_start("far", far, 0)
    arrive(st.zf[1])
    st.y_start("far", far, 1)

    own_as.wait()
    arrive(*as_2)

    def turn(i, carry):
        cols = pl.ds(pl.multiple_of(i * 128, 128), 128)
        block = as_buf[:, :, cols].reshape(512, 128).astype(F32)
        flat = block.T.astype(BF16)
        for yy in range(4):
            at = pl.multiple_of((yy * 4 + i) * 32, 32)
            as_t[pl.ds(at, 32)] = flat[yy * 32 : (yy + 1) * 32]
        return carry

    lax.fori_loop(0, 4, turn, 0)

    st.y_forward("far", far, 0)
    st.y_forward("far", far, 1)
    te.y_forward("prev", prev, 0)
    te.y_forward("next", nxt, 1)
    arrive(*st.last)
    for i in range(16):
        tall = bs_buf[i].astype(F32).reshape(4, 2, 8, 256)
        rows = slice(i * 32, (i + 1) * 32)
        bs_full[rows, :256] = tall[:, 0].reshape(32, 256).astype(BF16)
        bs_full[rows, 256:] = tall[:, 1].reshape(32, 256).astype(BF16)

    def student_part(out, slot):
        out[...] = jnp.dot(as_buf[slot], bs_full[...], preferred_element_type=F32)

    cs_swap = []
    for k in range(2):
        student_part(cs_send.at[k], (1 - c) * 2 + k)
        cs_swap.append(send(cs_send.at[k], cs_recv.at[k], dev(dc=1)))
    for k in range(2):
        student_part(cs_own.at[k], c * 2 + k)

    def tokens_of(ref, chip):
        return ref.at[lax.div(chip, 2), pl.ds(pl.multiple_of(lax.rem(chip, 2) * 64, 64), 64)]

    def pack(v):
        halves = []
        for w in (v[:, :256], v[:, 256:]):
            near = w.astype(BF16)
            wide = near.astype(F32)
            size = jnp.abs(wide)
            fits = size > 1e-30
            steps = (w - wide) * (1792.0 / jnp.where(fits, size, 1.0))
            halves.append((near, jnp.round(jnp.where(fits, steps, 0.0))))
        (n0, r0), (n1, r1) = halves
        return n0, n1, (16.0 * r0 + r1).astype(BF16)

    def unpack(ref):
        both = ref[:, 512:].astype(F32)
        r0 = jnp.round(both * 0.0625)
        out = []
        for i, r in enumerate((r0, both - 16.0 * r0)):
            wide = ref[:, i * 256 : (i + 1) * 256].astype(F32)
            out.append(wide + r * (jnp.abs(wide) * (1.0 / 1792.0)))
        return jnp.concatenate(out, axis=1)

    def scatter_z(swaps, own, recv, zsend, zrecv):
        arrive(*swaps)
        copies = []
        for d in (2, 1, 3, 0):
            mine, theirs = tokens_of(own, mod4(zl + d)), tokens_of(recv, mod4(zl + d))
            total = mine[...] + theirs[...]
            if d == 0:
                mine[...] = total
            else:
                for i, third in enumerate(pack(total)):
                    zsend[d - 1, :, i * 256 : (i + 1) * 256] = third
                copies.append(send(zsend.at[d - 1], zrecv.at[d - 1], dev(dzl=d)))
        return copies

    def teacher_part(out, slot, zi, first):
        a = at_buf[slot, :, pl.ds(pl.multiple_of(zi * 512, 512), 512)]
        b = bt_buf[pl.ds(zi * 4, 4)].reshape(512, 512)
        part = jnp.dot(a, b, preferred_element_type=F32)
        out[...] = part if first else out[...] + part

    def teacher_parts(zi, first):
        for k in range(2):
            teacher_part(ct_send.at[k], (1 - c) * 2 + k, zi, first)
            teacher_part(ct_own.at[k], c * 2 + k, zi, first)

    arrive(te.zs[1, 1])
    te.y_start("prev", prev, 1)
    arrive(te.zs[3, 0])
    te.y_start("next", nxt, 0)
    own_at.wait()
    arrive(*at_2)
    arrive(*te.last[:4])
    teacher_parts(zh, True)
    arrive(te.zf[0])
    te.y_start("far", far, 0)
    arrive(te.zf[1])
    te.y_start("far", far, 1)
    cs_z = scatter_z(cs_swap, cs_own, cs_recv, zs_send, zs_recv)
    te.y_forward("prev", prev, 1)
    te.y_forward("next", nxt, 0)
    te.y_forward("far", far, 0)
    te.y_forward("far", far, 1)
    arrive(*te.last[4:12])
    teacher_parts(prev, False)
    teacher_parts(nxt, False)
    arrive(*te.last[12:])

    ct_swap = []
    for k in range(2):
        teacher_part(ct_send.at[k], (1 - c) * 2 + k, far, False)
        ct_swap.append(send(ct_send.at[k], ct_recv.at[k], dev(dc=1)))
    for k in range(2):
        teacher_part(ct_own.at[k], c * 2 + k, far, False)
    ct_z = scatter_z(ct_swap, ct_own, ct_recv, zt_send, zt_recv)
    drain()

    def scaled(own, zrecv):
        return (tokens_of(own, zl)[...] + sum(unpack(zrecv.at[k]) for k in range(3))) * 0.5

    arrive(*cs_z)
    s = scaled(cs_own, zs_recv)
    ms = jnp.max(s, axis=-1, keepdims=True)
    es = jnp.sum(jnp.exp(s - ms), axis=-1, keepdims=True)
    arrive(*ct_z)
    t = scaled(ct_own, zt_recv)
    mt = jnp.max(t, axis=-1, keepdims=True)
    et = jnp.exp(t - mt)
    ws = jnp.sum(et * (t - s), axis=-1, keepdims=True)
    et = jnp.sum(et, axis=-1, keepdims=True)

    lane = lax.broadcasted_iota(jnp.int32, (64, 128), 1)
    stat = jnp.zeros((64, 128), F32)
    for i, col in enumerate((mt, et, ms, es, ws)):
        stat = jnp.where(lane == i, col, stat)
    flat = stat.T[:8]
    stat_buf[x] = jnp.concatenate([flat, flat], axis=1)
    stats = [send(stat_buf.at[x], stat_buf.at[x], dev(dx=d)) for d in (1, 3, 2)]
    arrive(*rests)
    arrive(*stats)
    got = [stat_buf[i] for i in range(4)]
    rests8 = rest_buf[c * 2 + lax.div(zl, 2)]

    def log_add(a, b):
        top = jnp.maximum(a, b)
        return top + jnp.log(jnp.exp(a - top) + jnp.exp(b - top))

    def whole(k):
        tops = [v[k : k + 1] for v in got]
        sums = [v[k + 1 : k + 2] for v in got]
        top = jnp.maximum(jnp.maximum(tops[0], tops[1]), jnp.maximum(tops[2], tops[3]))
        scale = [jnp.exp(m - top) for m in tops]
        total = sum(a * b for a, b in zip(sums, scale))
        return top, scale, total

    top_t, scale_t, sum_t = whole(0)
    top_s, _, sum_s = whole(2)
    norm_t = log_add(top_t + jnp.log(sum_t), rests8[0:1])
    norm_s = log_add(top_s + jnp.log(sum_s), rests8[1:2])
    upper = lax.rem(zl, 2)
    square = lax.broadcasted_iota(jnp.int32, (128, 128), 0)
    turned = jnp.where(square == 0, norm_t, norm_s).T
    turned = jnp.where(upper == 0, turned[:64], turned[64:])
    col_t, col_s = turned[:, 0:1], turned[:, 1:2]

    j = c * 4 + zl
    g_z, g_chip = [], []
    for v in range(2):
        cols = slice(v * 256, (v + 1) * 256)
        gap = jnp.exp(s[:, cols] - col_s) - jnp.exp(t[:, cols] - col_t)
        g_buf[v, j] = (8.0 * gap).astype(BF16)
        mine = g_buf.at[v, j]
        g_z.append([send(mine, mine, dev(dzl=d)) for d in (2, 1, 3)])
        g_chip.append(send(mine, mine, dev(dc=1)))

    weighted = sum(v[4:5] * b for v, b in zip(got, scale_t))
    inside = jnp.exp(top_t - norm_t)
    kl = 16.0 * (weighted * inside - sum_t * inside * (norm_t - norm_s))
    half_of = lax.div(lax.broadcasted_iota(jnp.int32, (1, 128), 1), 64)
    kl_buf[j] = jnp.broadcast_to(jnp.where(half_of == upper, kl, 0.0), (8, 128))
    kls = [
        send(kl_buf.at[j], kl_buf.at[j], dev(dzl=a, dc=b))
        for a in range(4)
        for b in range(2)
        if a + b > 0
    ]

    gw_c, gh_c = [], []
    for v in range(2):
        g_f = []
        for copy, d in zip(g_z[v], (2, 1, 3)):
            arrive(copy)
            theirs = g_buf.at[v, c * 4 + mod4(zl - d)]
            g_f.append(send(theirs, theirs, dev(dc=1)))
        arrive(g_chip[v], *g_f)

        g = g_buf[v].reshape(512, 256)
        sent = []
        for d in (2, 1, 3, 0):
            rows = pl.ds(pl.multiple_of(mod4(y + d) * 128, 128), 128)
            part = jnp.dot(as_t[rows], g, preferred_element_type=F32)
            if d == 0:
                gw_own[v] = part
            else:
                gw_send[v, d - 1] = part.astype(BF16)
                sent.append(send(gw_send.at[v, d - 1], gw_recv.at[v, d - 1], dev(dy=d)))
        gw_c.append(sent)

        for d in (2, 1, 3, 0):
            rows = g_buf[v, pl.ds(mod4(x + d) * 2, 2)].reshape(128, 256)
            part = lax.dot_general(
                rows,
                bs_full[:, v * 256 : (v + 1) * 256],
                (((1,), (1,)), ((), ())),
                preferred_element_type=F32,
            )
            if v == 0:
                gh_own[d] = part
            elif d == 0:
                gh_own[0] = gh_own[0] + part
            else:
                gh_send[d - 1] = (gh_own[d] + part).astype(BF16)
                gh_c.append(send(gh_send.at[d - 1], gh_recv.at[d - 1], dev(dx=d)))

    w_c = []
    for v in range(2):
        arrive(*gw_c[v])
        total = gw_own[v] + sum(gw_recv[v, k].astype(F32) for k in range(3))
        total = total.reshape(4, 32, 256)
        w_own[v] = total
        w_send[v] = total.astype(BF16)
        w_c.append(
            [
                send(w_send.at[v, mod4(zh + d)], w_recv.at[v, d - 1], dev(dzh=d))
                for d in (2, 1, 3)
            ]
        )

    def write_out(src, dst, k):
        copy = pltpu.make_async_copy(src, dst, local_sem.at[k])
        copy.start()
        return copy

    arrive(*gh_c)
    gh_vmem[...] = gh_own[0] + sum(gh_recv[k].astype(F32) for k in range(3))
    outs = [write_out(gh_vmem, gh_out, 6)]
    arrive(*kls)
    k0 = lax.div(x, 2) * 4 + lax.rem(x, 2) * 2
    kl_vmem[...] = kl_buf[k0, 0:1] + kl_buf[k0 + 1, 0:1]
    outs.append(write_out(kl_vmem, kl_out, 7))

    x_c = []
    for v in range(2):
        arrive(*w_c[v])
        rows = w_own[v, zh] + sum(w_recv[v, k].astype(F32) for k in range(3))
        x_send[v] = rows.reshape(4, 8, 256)
        cols = pl.ds(pl.multiple_of(x * 512 + v * 256, 256), 256)
        gw_vmem[:, cols] = x_send[v, x]
        x_c += [
            send(x_send.at[v, mod4(x + d)], gw_vmem.at[:, cols], dev(dx=d))
            for d in (2, 1, 3)
        ]
    drain()
    arrive(*x_c)
    outs.append(write_out(gw_vmem, gw_out, 8))
    for copy in outs:
        copy.wait()


def settle_kernel(kl_in, gw_in, gh_in, kl_out, gw_out, gh_out, kl_vmem, gw_vmem, gh_vmem, sem):
    ways = ((gh_in, gh_vmem, gh_out), (gw_in, gw_vmem, gw_out), (kl_in, kl_vmem, kl_out))
    into = [pltpu.make_async_copy(a, b, sem.at[i]) for i, (a, b, _) in enumerate(ways)]
    onto = [pltpu.make_async_copy(b, o, sem.at[3 + i]) for i, (_, b, o) in enumerate(ways)]
    for copy in into:
        copy.start()
    for first, then in zip(into, onto):
        first.wait()
        then.start()
    for copy in onto:
        copy.wait()


def body(teacher_hidden, teacher_head, student_hidden, student_head, teacher_rest, student_rest):
    hbm = pl.BlockSpec(memory_space=pltpu.HBM)
    out_shape = (
        jax.ShapeDtypeStruct((1, 128), F32),
        jax.ShapeDtypeStruct((8, 2048), F32),
        jax.ShapeDtypeStruct((128, 512), F32),
    )
    results = pl.pallas_call(
        distill_kernel,
        out_shape=out_shape,
        in_specs=[hbm] * 6,
        out_specs=(hbm, hbm, hbm),
        scratch_shapes=[
            pltpu.VMEM((8, 2048), BF16),
            pltpu.VMEM((1, 128), F32),
            pltpu.VMEM((1, 128), F32),
            pltpu.VMEM((4, 16, 256), BF16),
            pltpu.VMEM((8, 128), F32),
            pltpu.VMEM((4, 128, 2048), BF16),
            pltpu.VMEM((4, 128, 512), BF16),
            pltpu.VMEM((16, 128, 512), BF16),
            pltpu.VMEM((16, 64, 256), BF16),
            pltpu.VMEM((512, 512), BF16),
            pltpu.VMEM((512, 512), BF16),
            pltpu.VMEM((4, 8, 128), F32),
            pltpu.VMEM((2, 128, 512), F32),
            pltpu.VMEM((2, 128, 512), F32),
            pltpu.VMEM((2, 128, 512), F32),
            pltpu.VMEM((2, 128, 512), F32),
            pltpu.VMEM((2, 128, 512), F32),
            pltpu.VMEM((2, 128, 512), F32),
            pltpu.VMEM((3, 64, 768), BF16),
            pltpu.VMEM((3, 64, 768), BF16),
            pltpu.VMEM((3, 64, 768), BF16),
            pltpu.VMEM((3, 64, 768), BF16),
            pltpu.VMEM((4, 8, 128), F32),
            pltpu.VMEM((2, 8, 64, 256), BF16),
            pltpu.VMEM((8, 8, 128), F32),
            pltpu.VMEM((4, 128, 512), F32),
            pltpu.VMEM((3, 128, 512), BF16),
            pltpu.VMEM((3, 128, 512), BF16),
            pltpu.VMEM((2, 128, 256), F32),
            pltpu.VMEM((2, 3, 128, 256), BF16),
            pltpu.VMEM((2, 3, 128, 256), BF16),
            pltpu.VMEM((2, 4, 32, 256), F32),
            pltpu.VMEM((2, 4, 32, 256), BF16),
            pltpu.VMEM((2, 3, 32, 256), BF16),
            pltpu.VMEM((2, 4, 8, 256), F32),
            pltpu.VMEM((1, 128), F32),
            pltpu.VMEM((8, 2048), F32),
            pltpu.VMEM((128, 512), F32),
            pltpu.SemaphoreType.DMA((N_COPY,)),
            pltpu.SemaphoreType.DMA((N_COPY,)),
            pltpu.SemaphoreType.DMA((9,)),
        ],
        compiler_params=pltpu.CompilerParams(
            collective_id=0, has_side_effects=True, vmem_limit_bytes=63 * 1024 * 1024
        ),
    )(
        teacher_hidden,
        teacher_head,
        student_hidden,
        student_head,
        teacher_rest.reshape(1, 128),
        student_rest.reshape(1, 128),
    )
    kl, grad_head, grad_hidden = pl.pallas_call(
        settle_kernel,
        out_shape=out_shape,
        in_specs=[hbm] * 3,
        out_specs=(hbm, hbm, hbm),
        scratch_shapes=[
            pltpu.VMEM((1, 128), F32),
            pltpu.VMEM((8, 2048), F32),
            pltpu.VMEM((128, 512), F32),
            pltpu.SemaphoreType.DMA((6,)),
        ],
        compiler_params=pltpu.CompilerParams(vmem_limit_bytes=63 * 1024 * 1024),
    )(*results)
    return kl.reshape(128), grad_head, grad_hidden


def solution(mesh):
    return jax.shard_map(
        body,
        mesh=mesh,
        in_specs=(
            P("fsdp", "role"),
            P(("role", "fsdp"), None),
            P("fsdp", "role"),
            P(("role", "fsdp"), None),
            P("fsdp"),
            P("fsdp"),
        ),
        out_specs=(P("fsdp"), P(("role", "fsdp"), None), P("fsdp", "role")),
        check_vma=False,
    )
```

```python
import jax
import jax.numpy as jnp
from jax import lax
from jax.experimental import pallas as pl
from jax.experimental.pallas import tpu as pltpu
from jax.sharding import PartitionSpec as P

MESH = pl.DeviceIdType.MESH
F32 = jnp.float32
BF16 = jnp.bfloat16
N_COPY = 144


def mod4(v):
    return lax.rem(v + 8, 4)


def distill_kernel(
    at_hbm,
    bt_hbm,
    as_hbm,
    sh_hbm,
    tr_hbm,
    sr_hbm,
    kl_out,
    gw_out,
    gh_out,
    sh_ref,
    tr_ref,
    sr_ref,
    bs_src,
    rest_src,
    at_buf,
    as_buf,
    bt_buf,
    bs_buf,
    bs_full,
    as_t,
    rest_buf,
    ct_send,
    ct_recv,
    ct_own,
    cs_send,
    cs_recv,
    cs_own,
    zt_recv,
    zs_recv,
    stat_buf,
    g_buf,
    kl_buf,
    gh_own,
    gh_send,
    gh_recv,
    gw_own,
    gw_send,
    gw_recv,
    w_own,
    w_send,
    w_recv,
    x_send,
    kl_vmem,
    gw_vmem,
    gh_vmem,
    send_sem,
    recv_sem,
    local_sem,
):
    role = lax.axis_index("role")
    fsdp = lax.axis_index("fsdp")
    zl, c = lax.div(role, 2), lax.rem(role, 2)
    zh, y, x = lax.div(fsdp, 16), lax.rem(lax.div(fsdp, 4), 4), lax.rem(fsdp, 4)

    def dev(dzl=0, dc=0, dzh=0, dy=0, dx=0):
        r = mod4(zl + dzl) * 2 + lax.rem(c + dc, 2)
        f = (mod4(zh + dzh) * 4 + mod4(y + dy)) * 4 + mod4(x + dx)
        return (r, f)

    started, pending = [], []

    def send(src, dst, to):
        k = len(started)
        copy = pltpu.make_async_remote_copy(
            src_ref=src,
            dst_ref=dst,
            send_sem=send_sem.at[k],
            recv_sem=recv_sem.at[k],
            device_id=to,
            device_id_type=MESH,
        )
        copy.start()
        started.append(copy)
        pending.append(copy)
        return copy

    def drain():
        while pending:
            pending.pop(0).wait_send()

    def arrive(*copies):
        for copy in copies:
            copy.wait_recv()

    partners = [dev(dzh=d) for d in (1, 2, 3)] + [dev(dx=d) for d in (1, 2, 3)]
    partners += [dev(dy=d) for d in (1, 2, 3)]
    partners += [dev(dzl=a, dc=b) for a in range(4) for b in range(2) if a + b > 0]
    barrier = pltpu.get_barrier_semaphore()
    for to in partners:
        pl.semaphore_signal(barrier, inc=1, device_id=to, device_id_type=MESH)

    own_at = pltpu.make_async_copy(at_hbm, at_buf.at[x], local_sem.at[0])
    own_as = pltpu.make_async_copy(as_hbm, as_buf.at[x], local_sem.at[1])
    piece = zh * 4 + y
    row32 = pl.multiple_of(x * 32, 32)
    row16 = pl.multiple_of(x * 16, 16)
    own_bt = pltpu.make_async_copy(
        bt_hbm.at[:, pl.ds(pl.multiple_of(x * 512, 512), 512)],
        bt_buf.at[piece, pl.ds(row32, 32)],
        local_sem.at[2],
    )
    small = [
        pltpu.make_async_copy(src, dst, local_sem.at[3 + i])
        for i, (src, dst) in enumerate(
            ((sh_hbm, sh_ref), (tr_hbm, tr_ref), (sr_hbm, sr_ref))
        )
    ]
    for copy in small:
        copy.start()
    own_bt.start()
    own_as.start()
    own_at.start()
    for copy in small:
        copy.wait()

    for q in range(4):
        wide = sh_ref[:, q * 512 : (q + 1) * 512].astype(F32)
        bs_src[q] = jnp.concatenate([wide[:, :256], wide[:, 256:]], axis=0).astype(BF16)
    bs_buf[piece, pl.ds(row16, 16)] = bs_src[x]
    r8 = lax.broadcasted_iota(jnp.int32, (8, 128), 0)
    rest = jnp.where(r8 == 0, tr_ref[...], jnp.where(r8 == 1, sr_ref[...], 0.0))
    rest_src[...] = rest
    rest_buf[x] = rest

    pl.semaphore_wait(barrier, len(partners))

    bs_a2a, bt_a2a = [], []
    for d in (1, 3, 2):
        q = mod4(x + d)
        bs_a2a.append(send(bs_src.at[q], bs_buf.at[piece, pl.ds(row16, 16)], dev(dx=d)))
    for d in (1, 3, 2):
        q = mod4(x + d)
        bt_a2a.append(
            send(
                bt_hbm.at[:, pl.ds(pl.multiple_of(q * 512, 512), 512)],
                bt_buf.at[piece, pl.ds(row32, 32)],
                dev(dx=d),
            )
        )
    rests = [send(rest_src, rest_buf.at[x], dev(dx=d)) for d in (1, 3, 2)]

    order = ((1, 0), (3, 1), (1, 1), (3, 0))

    def unit(buf, i, h, rows):
        return buf.at[i, pl.ds(h * rows, rows)]

    def pass_on(buf, i, h, rows, to):
        ref = unit(buf, i, h, rows)
        return send(ref, ref, to)

    def x_start(src, buf):
        return {
            (d, h): send(src.at[pl.ds(h * 64, 64)], unit(buf, x, h, 64), dev(dx=d))
            for d, h in order
        }

    def x_forward(sent, buf):
        arrive(sent[1, 0])
        a = pass_on(buf, mod4(x - 1), 0, 64, dev(dx=1))
        arrive(sent[3, 1])
        b = pass_on(buf, mod4(x + 1), 1, 64, dev(dx=3))
        return [sent[1, 1], sent[3, 0], a, b]

    class Head:
        def __init__(self, buf, rows):
            self.buf, self.rows = buf, rows
            self.zs, self.ys, self.last = {}, {}, []

        def z_start(self, which):
            for d, h in which:
                self.zs[d, h] = pass_on(self.buf, piece, h, self.rows, dev(dzh=d))

        def z_forward(self):
            arrive(self.zs[1, 0])
            a = pass_on(self.buf, prev * 4 + y, 0, self.rows, dev(dzh=1))
            arrive(self.zs[3, 1])
            b = pass_on(self.buf, nxt * 4 + y, 1, self.rows, dev(dzh=3))
            self.zf = (a, b)

        def y_start(self, name, zi, h):
            for d in (1, 3):
                self.ys[name, h, d] = pass_on(
                    self.buf, zi * 4 + y, h, self.rows, dev(dy=d)
                )

        def y_forward(self, name, zi, h):
            d = 1 if h == 0 else 3
            arrive(self.ys[name, h, d])
            i = zi * 4 + mod4(y - 1 if h == 0 else y + 1)
            self.last.append(pass_on(self.buf, i, h, self.rows, dev(dy=d)))
            self.last.append(self.ys[name, h, 4 - d])

    prev, nxt, far = mod4(zh - 1), mod4(zh + 1), mod4(zh + 2)
    te = Head(bt_buf, 64)

    as_1 = x_start(as_hbm, as_buf)
    at_1 = x_start(at_hbm, at_buf)

    def y_direct(zi):
        ref = bs_buf.at[zi * 4 + y]
        return [send(ref, ref, dev(dy=d)) for d in (1, 3, 2)]

    arrive(*bs_a2a)
    st_z = [send(bs_buf.at[piece], bs_buf.at[piece], dev(dzh=d)) for d in (1, 3)]
    st_y = y_direct(zh)
    own_bt.wait()
    arrive(*bt_a2a)
    te.z_start(order[:2])
    te.y_start("own", zh, 0)
    te.y_start("own", zh, 1)
    as_2 = x_forward(as_1, as_buf)
    arrive(st_z[0])
    st_f = [pass_on(bs_buf, prev * 4 + y, 0, 32, dev(dzh=1))]
    arrive(st_z[1])
    st_f.append(pass_on(bs_buf, nxt * 4 + y, 1, 32, dev(dzh=3)))
    te.z_start(order[2:])
    st_y += y_direct(prev)
    st_y += y_direct(nxt)
    te.y_forward("own", zh, 0)
    te.y_forward("own", zh, 1)
    arrive(*st_f)
    st_y += y_direct(far)
    at_2 = x_forward(at_1, at_buf)
    te.z_forward()
    te.y_start("prev", prev, 0)
    te.y_start("next", nxt, 1)

    own_as.wait()
    arrive(*as_2)

    def turn(i, carry):
        cols = pl.ds(pl.multiple_of(i * 128, 128), 128)
        block = as_buf[:, :, cols].reshape(512, 128).astype(F32)
        flat = block.T.astype(BF16)
        for yy in range(4):
            at = pl.multiple_of((yy * 4 + i) * 32, 32)
            as_t[pl.ds(at, 32)] = flat[yy * 32 : (yy + 1) * 32]
        return carry

    lax.fori_loop(0, 4, turn, 0)

    te.y_forward("prev", prev, 0)
    te.y_forward("next", nxt, 1)
    arrive(*st_y)
    for i in range(16):
        tall = bs_buf[i].astype(F32).reshape(4, 2, 8, 256)
        rows = slice(i * 32, (i + 1) * 32)
        bs_full[rows, :256] = tall[:, 0].reshape(32, 256).astype(BF16)
        bs_full[rows, 256:] = tall[:, 1].reshape(32, 256).astype(BF16)

    def student_part(out, slot):
        out[...] = jnp.dot(as_buf[slot], bs_full[...], preferred_element_type=F32)

    cs_swap = []
    for k in range(2):
        student_part(cs_send.at[k], (1 - c) * 2 + k)
        cs_swap.append(send(cs_send.at[k], cs_recv.at[k], dev(dc=1)))
    for k in range(2):
        student_part(cs_own.at[k], c * 2 + k)

    def tokens_of(ref, chip):
        return ref.at[lax.div(chip, 2), pl.ds(pl.multiple_of(lax.rem(chip, 2) * 64, 64), 64)]

    def scatter_z(swaps, own, recv, zrecv):
        arrive(*swaps)
        copies = []
        for d in (2, 1, 3, 0):
            mine, theirs = tokens_of(own, mod4(zl + d)), tokens_of(recv, mod4(zl + d))
            mine[...] = mine[...] + theirs[...]
            if d > 0:
                copies.append(send(mine, zrecv.at[d - 1], dev(dzl=d)))
        return copies

    def teacher_part(out, slot, zi, first):
        a = at_buf[slot, :, pl.ds(pl.multiple_of(zi * 512, 512), 512)]
        b = bt_buf[pl.ds(zi * 4, 4)].reshape(512, 512)
        part = jnp.dot(a, b, preferred_element_type=F32)
        out[...] = part if first else out[...] + part

    def teacher_parts(zi, first):
        for k in range(2):
            teacher_part(ct_send.at[k], (1 - c) * 2 + k, zi, first)
            teacher_part(ct_own.at[k], c * 2 + k, zi, first)

    arrive(te.zs[1, 1])
    te.y_start("prev", prev, 1)
    arrive(te.zs[3, 0])
    te.y_start("next", nxt, 0)
    own_at.wait()
    arrive(*at_2)
    arrive(*te.last[:4])
    teacher_parts(zh, True)
    arrive(te.zf[0])
    te.y_start("far", far, 0)
    arrive(te.zf[1])
    te.y_start("far", far, 1)
    cs_z = scatter_z(cs_swap, cs_own, cs_recv, zs_recv)
    te.y_forward("prev", prev, 1)
    te.y_forward("next", nxt, 0)
    te.y_forward("far", far, 0)
    te.y_forward("far", far, 1)
    arrive(*te.last[4:12])
    teacher_parts(prev, False)
    teacher_parts(nxt, False)
    arrive(*te.last[12:])

    ct_swap = []
    for k in range(2):
        teacher_part(ct_send.at[k], (1 - c) * 2 + k, far, False)
        ct_swap.append(send(ct_send.at[k], ct_recv.at[k], dev(dc=1)))
    for k in range(2):
        teacher_part(ct_own.at[k], c * 2 + k, far, False)
    ct_z = scatter_z(ct_swap, ct_own, ct_recv, zt_recv)
    drain()

    def scaled(own, zrecv):
        return (tokens_of(own, zl)[...] + zrecv[0] + zrecv[1] + zrecv[2]) * 0.5

    arrive(*cs_z)
    s = scaled(cs_own, zs_recv)
    ms = jnp.max(s, axis=-1, keepdims=True)
    es = jnp.sum(jnp.exp(s - ms), axis=-1, keepdims=True)
    arrive(*ct_z)
    t = scaled(ct_own, zt_recv)
    mt = jnp.max(t, axis=-1, keepdims=True)
    et = jnp.exp(t - mt)
    ws = jnp.sum(et * (t - s), axis=-1, keepdims=True)
    et = jnp.sum(et, axis=-1, keepdims=True)

    lane = lax.broadcasted_iota(jnp.int32, (64, 128), 1)
    stat = jnp.zeros((64, 128), F32)
    for i, col in enumerate((mt, et, ms, es, ws)):
        stat = jnp.where(lane == i, col, stat)
    flat = stat.T[:8]
    stat_buf[x] = jnp.concatenate([flat, flat], axis=1)
    stats = [send(stat_buf.at[x], stat_buf.at[x], dev(dx=d)) for d in (1, 3, 2)]
    arrive(*rests)
    arrive(*stats)
    got = [stat_buf[i] for i in range(4)]
    rests8 = rest_buf[c * 2 + lax.div(zl, 2)]

    def log_add(a, b):
        top = jnp.maximum(a, b)
        return top + jnp.log(jnp.exp(a - top) + jnp.exp(b - top))

    def whole(k):
        tops = [v[k : k + 1] for v in got]
        sums = [v[k + 1 : k + 2] for v in got]
        top = jnp.maximum(jnp.maximum(tops[0], tops[1]), jnp.maximum(tops[2], tops[3]))
        scale = [jnp.exp(m - top) for m in tops]
        total = sum(a * b for a, b in zip(sums, scale))
        return top, scale, total

    top_t, scale_t, sum_t = whole(0)
    top_s, _, sum_s = whole(2)
    norm_t = log_add(top_t + jnp.log(sum_t), rests8[0:1])
    norm_s = log_add(top_s + jnp.log(sum_s), rests8[1:2])
    upper = lax.rem(zl, 2)
    square = lax.broadcasted_iota(jnp.int32, (128, 128), 0)
    turned = jnp.where(square == 0, norm_t, norm_s).T
    turned = jnp.where(upper == 0, turned[:64], turned[64:])
    col_t, col_s = turned[:, 0:1], turned[:, 1:2]

    j = c * 4 + zl
    g_z, g_chip = [], []
    for v in range(2):
        cols = slice(v * 256, (v + 1) * 256)
        gap = jnp.exp(s[:, cols] - col_s) - jnp.exp(t[:, cols] - col_t)
        g_buf[v, j] = (8.0 * gap).astype(BF16)
        mine = g_buf.at[v, j]
        g_z.append([send(mine, mine, dev(dzl=d)) for d in (2, 1, 3)])
        g_chip.append(send(mine, mine, dev(dc=1)))

    weighted = sum(v[4:5] * b for v, b in zip(got, scale_t))
    inside = jnp.exp(top_t - norm_t)
    kl = 16.0 * (weighted * inside - sum_t * inside * (norm_t - norm_s))
    half_of = lax.div(lax.broadcasted_iota(jnp.int32, (1, 128), 1), 64)
    kl_buf[j] = jnp.broadcast_to(jnp.where(half_of == upper, kl, 0.0), (8, 128))
    kls = [
        send(kl_buf.at[j], kl_buf.at[j], dev(dzl=a, dc=b))
        for a in range(4)
        for b in range(2)
        if a + b > 0
    ]

    gw_c, gh_c = [], []
    for v in range(2):
        g_f = []
        for copy, d in zip(g_z[v], (2, 1, 3)):
            arrive(copy)
            theirs = g_buf.at[v, c * 4 + mod4(zl - d)]
            g_f.append(send(theirs, theirs, dev(dc=1)))
        arrive(g_chip[v], *g_f)

        g = g_buf[v].reshape(512, 256)
        sent = []
        for d in (2, 1, 3, 0):
            rows = pl.ds(pl.multiple_of(mod4(y + d) * 128, 128), 128)
            part = jnp.dot(as_t[rows], g, preferred_element_type=F32)
            if d == 0:
                gw_own[v] = part
            else:
                gw_send[v, d - 1] = part.astype(BF16)
                sent.append(send(gw_send.at[v, d - 1], gw_recv.at[v, d - 1], dev(dy=d)))
        gw_c.append(sent)

        for d in (2, 1, 3, 0):
            rows = g_buf[v, pl.ds(mod4(x + d) * 2, 2)].reshape(128, 256)
            part = lax.dot_general(
                rows,
                bs_full[:, v * 256 : (v + 1) * 256],
                (((1,), (1,)), ((), ())),
                preferred_element_type=F32,
            )
            if v == 0:
                gh_own[d] = part
            elif d == 0:
                gh_own[0] = gh_own[0] + part
            else:
                gh_send[d - 1] = (gh_own[d] + part).astype(BF16)
                gh_c.append(send(gh_send.at[d - 1], gh_recv.at[d - 1], dev(dx=d)))

    w_c = []
    for v in range(2):
        arrive(*gw_c[v])
        total = gw_own[v] + sum(gw_recv[v, k].astype(F32) for k in range(3))
        total = total.reshape(4, 32, 256)
        w_own[v] = total
        w_send[v] = total.astype(BF16)
        w_c.append(
            [
                send(w_send.at[v, mod4(zh + d)], w_recv.at[v, d - 1], dev(dzh=d))
                for d in (2, 1, 3)
            ]
        )

    def write_out(src, dst, k):
        copy = pltpu.make_async_copy(src, dst, local_sem.at[k])
        copy.start()
        return copy

    arrive(*gh_c)
    gh_vmem[...] = gh_own[0] + sum(gh_recv[k].astype(F32) for k in range(3))
    outs = [write_out(gh_vmem, gh_out, 6)]
    arrive(*kls)
    k0 = lax.div(x, 2) * 4 + lax.rem(x, 2) * 2
    kl_vmem[...] = kl_buf[k0, 0:1] + kl_buf[k0 + 1, 0:1]
    outs.append(write_out(kl_vmem, kl_out, 7))

    x_c = []
    for v in range(2):
        arrive(*w_c[v])
        rows = w_own[v, zh] + sum(w_recv[v, k].astype(F32) for k in range(3))
        x_send[v] = rows.reshape(4, 8, 256)
        cols = pl.ds(pl.multiple_of(x * 512 + v * 256, 256), 256)
        gw_vmem[:, cols] = x_send[v, x]
        x_c += [
            send(x_send.at[v, mod4(x + d)], gw_vmem.at[:, cols], dev(dx=d))
            for d in (2, 1, 3)
        ]
    drain()
    arrive(*x_c)
    outs.append(write_out(gw_vmem, gw_out, 8))
    for copy in outs:
        copy.wait()


def settle_kernel(kl_in, gw_in, gh_in, kl_out, gw_out, gh_out, kl_vmem, gw_vmem, gh_vmem, sem):
    ways = ((gh_in, gh_vmem, gh_out), (gw_in, gw_vmem, gw_out), (kl_in, kl_vmem, kl_out))
    into = [pltpu.make_async_copy(a, b, sem.at[i]) for i, (a, b, _) in enumerate(ways)]
    onto = [pltpu.make_async_copy(b, o, sem.at[3 + i]) for i, (_, b, o) in enumerate(ways)]
    for copy in into:
        copy.start()
    for first, then in zip(into, onto):
        first.wait()
        then.start()
    for copy in onto:
        copy.wait()


def body(teacher_hidden, teacher_head, student_hidden, student_head, teacher_rest, student_rest):
    hbm = pl.BlockSpec(memory_space=pltpu.HBM)
    out_shape = (
        jax.ShapeDtypeStruct((1, 128), F32),
        jax.ShapeDtypeStruct((8, 2048), F32),
        jax.ShapeDtypeStruct((128, 512), F32),
    )
    results = pl.pallas_call(
        distill_kernel,
        out_shape=out_shape,
        in_specs=[hbm] * 6,
        out_specs=(hbm, hbm, hbm),
        scratch_shapes=[
            pltpu.VMEM((8, 2048), BF16),
            pltpu.VMEM((1, 128), F32),
            pltpu.VMEM((1, 128), F32),
            pltpu.VMEM((4, 16, 256), BF16),
            pltpu.VMEM((8, 128), F32),
            pltpu.VMEM((4, 128, 2048), BF16),
            pltpu.VMEM((4, 128, 512), BF16),
            pltpu.VMEM((16, 128, 512), BF16),
            pltpu.VMEM((16, 64, 256), BF16),
            pltpu.VMEM((512, 512), BF16),
            pltpu.VMEM((512, 512), BF16),
            pltpu.VMEM((4, 8, 128), F32),
            pltpu.VMEM((2, 128, 512), F32),
            pltpu.VMEM((2, 128, 512), F32),
            pltpu.VMEM((2, 128, 512), F32),
            pltpu.VMEM((2, 128, 512), F32),
            pltpu.VMEM((2, 128, 512), F32),
            pltpu.VMEM((2, 128, 512), F32),
            pltpu.VMEM((3, 64, 512), F32),
            pltpu.VMEM((3, 64, 512), F32),
            pltpu.VMEM((4, 8, 128), F32),
            pltpu.VMEM((2, 8, 64, 256), BF16),
            pltpu.VMEM((8, 8, 128), F32),
            pltpu.VMEM((4, 128, 512), F32),
            pltpu.VMEM((3, 128, 512), BF16),
            pltpu.VMEM((3, 128, 512), BF16),
            pltpu.VMEM((2, 128, 256), F32),
            pltpu.VMEM((2, 3, 128, 256), BF16),
            pltpu.VMEM((2, 3, 128, 256), BF16),
            pltpu.VMEM((2, 4, 32, 256), F32),
            pltpu.VMEM((2, 4, 32, 256), BF16),
            pltpu.VMEM((2, 3, 32, 256), BF16),
            pltpu.VMEM((2, 4, 8, 256), F32),
            pltpu.VMEM((1, 128), F32),
            pltpu.VMEM((8, 2048), F32),
            pltpu.VMEM((128, 512), F32),
            pltpu.SemaphoreType.DMA((N_COPY,)),
            pltpu.SemaphoreType.DMA((N_COPY,)),
            pltpu.SemaphoreType.DMA((9,)),
        ],
        compiler_params=pltpu.CompilerParams(
            collective_id=0, has_side_effects=True, vmem_limit_bytes=63 * 1024 * 1024
        ),
    )(
        teacher_hidden,
        teacher_head,
        student_hidden,
        student_head,
        teacher_rest.reshape(1, 128),
        student_rest.reshape(1, 128),
    )
    kl, grad_head, grad_hidden = pl.pallas_call(
        settle_kernel,
        out_shape=out_shape,
        in_specs=[hbm] * 3,
        out_specs=(hbm, hbm, hbm),
        scratch_shapes=[
            pltpu.VMEM((1, 128), F32),
            pltpu.VMEM((8, 2048), F32),
            pltpu.VMEM((128, 512), F32),
            pltpu.SemaphoreType.DMA((6,)),
        ],
        compiler_params=pltpu.CompilerParams(vmem_limit_bytes=63 * 1024 * 1024),
    )(*results)
    return kl.reshape(128), grad_head, grad_hidden


def solution(mesh):
    return jax.shard_map(
        body,
        mesh=mesh,
        in_specs=(
            P("fsdp", "role"),
            P(("role", "fsdp"), None),
            P("fsdp", "role"),
            P(("role", "fsdp"), None),
            P("fsdp"),
            P("fsdp"),
        ),
        out_specs=(P("fsdp"), P(("role", "fsdp"), None), P("fsdp", "role")),
        check_vma=False,
    )
```

```python
import jax
import jax.numpy as jnp
from jax import lax
from jax.experimental import pallas as pl
from jax.experimental.pallas import tpu as pltpu
from jax.sharding import PartitionSpec as P

MESH = pl.DeviceIdType.MESH
F32 = jnp.float32
BF16 = jnp.bfloat16
N_COPY = 176


def mod4(v):
    return lax.rem(v + 8, 4)


def distill_kernel(
    at_hbm,
    bt_hbm,
    as_hbm,
    sh_hbm,
    tr_hbm,
    sr_hbm,
    kl_out,
    gw_out,
    gh_out,
    sh_ref,
    tr_ref,
    sr_ref,
    bs_src,
    rest_src,
    at_buf,
    as_buf,
    bt_buf,
    bs_buf,
    bs_full,
    as_t,
    rest_buf,
    ct_send,
    ct_recv,
    ct_own,
    cs_send,
    cs_recv,
    cs_own,
    zt_recv,
    zs_recv,
    stat_buf,
    g_buf,
    kl_buf,
    gh_own,
    gh_send,
    gh_recv,
    gw_own,
    gw_send,
    gw_recv,
    w_own,
    w_send,
    w_recv,
    x_send,
    kl_vmem,
    gw_vmem,
    gh_vmem,
    send_sem,
    recv_sem,
    local_sem,
):
    role = lax.axis_index("role")
    fsdp = lax.axis_index("fsdp")
    zl, c = lax.div(role, 2), lax.rem(role, 2)
    zh, y, x = lax.div(fsdp, 16), lax.rem(lax.div(fsdp, 4), 4), lax.rem(fsdp, 4)

    def dev(dzl=0, dc=0, dzh=0, dy=0, dx=0):
        r = mod4(zl + dzl) * 2 + lax.rem(c + dc, 2)
        f = (mod4(zh + dzh) * 4 + mod4(y + dy)) * 4 + mod4(x + dx)
        return (r, f)

    started, pending = [], []

    def send(src, dst, to):
        k = len(started)
        copy = pltpu.make_async_remote_copy(
            src_ref=src,
            dst_ref=dst,
            send_sem=send_sem.at[k],
            recv_sem=recv_sem.at[k],
            device_id=to,
            device_id_type=MESH,
        )
        copy.start()
        started.append(copy)
        pending.append(copy)
        return copy

    def drain():
        while pending:
            pending.pop(0).wait_send()

    def arrive(*copies):
        for copy in copies:
            copy.wait_recv()

    partners = [dev(dzh=d) for d in (1, 2, 3)] + [dev(dx=d) for d in (1, 2, 3)]
    partners += [dev(dy=d) for d in (1, 2, 3)]
    partners += [dev(dzl=a, dc=b) for a in range(4) for b in range(2) if a + b > 0]
    barrier = pltpu.get_barrier_semaphore()
    for to in partners:
        pl.semaphore_signal(barrier, inc=1, device_id=to, device_id_type=MESH)

    own_at = pltpu.make_async_copy(at_hbm, at_buf.at[x], local_sem.at[0])
    own_as = pltpu.make_async_copy(as_hbm, as_buf.at[x], local_sem.at[1])
    piece = zh * 4 + y
    row32 = pl.multiple_of(x * 32, 32)
    row16 = pl.multiple_of(x * 16, 16)
    own_bt = pltpu.make_async_copy(
        bt_hbm.at[:, pl.ds(pl.multiple_of(x * 512, 512), 512)],
        bt_buf.at[piece, pl.ds(row32, 32)],
        local_sem.at[2],
    )
    small = [
        pltpu.make_async_copy(src, dst, local_sem.at[3 + i])
        for i, (src, dst) in enumerate(
            ((sh_hbm, sh_ref), (tr_hbm, tr_ref), (sr_hbm, sr_ref))
        )
    ]
    for copy in small:
        copy.start()
    own_bt.start()
    own_as.start()
    own_at.start()
    for copy in small:
        copy.wait()

    for q in range(4):
        wide = sh_ref[:, q * 512 : (q + 1) * 512].astype(F32)
        bs_src[q] = jnp.concatenate([wide[:, :256], wide[:, 256:]], axis=0).astype(BF16)
    bs_buf[piece, pl.ds(row16, 16)] = bs_src[x]
    r8 = lax.broadcasted_iota(jnp.int32, (8, 128), 0)
    rest = jnp.where(r8 == 0, tr_ref[...], jnp.where(r8 == 1, sr_ref[...], 0.0))
    rest_src[...] = rest
    rest_buf[x] = rest

    pl.semaphore_wait(barrier, len(partners))

    bs_a2a, bt_a2a = [], []
    for d in (1, 3, 2):
        q = mod4(x + d)
        bs_a2a.append(send(bs_src.at[q], bs_buf.at[piece, pl.ds(row16, 16)], dev(dx=d)))
    for d in (1, 3, 2):
        q = mod4(x + d)
        bt_a2a.append(
            send(
                bt_hbm.at[:, pl.ds(pl.multiple_of(q * 512, 512), 512)],
                bt_buf.at[piece, pl.ds(row32, 32)],
                dev(dx=d),
            )
        )
    rests = [send(rest_src, rest_buf.at[x], dev(dx=d)) for d in (1, 3, 2)]

    order = ((1, 0), (3, 1), (1, 1), (3, 0))

    def unit(buf, i, h, rows):
        return buf.at[i, pl.ds(h * rows, rows)]

    def pass_on(buf, i, h, rows, to):
        ref = unit(buf, i, h, rows)
        return send(ref, ref, to)

    def x_start(src, buf):
        return {
            (d, h): send(src.at[pl.ds(h * 64, 64)], unit(buf, x, h, 64), dev(dx=d))
            for d, h in order
        }

    def x_forward(sent, buf):
        arrive(sent[1, 0])
        a = pass_on(buf, mod4(x - 1), 0, 64, dev(dx=1))
        arrive(sent[3, 1])
        b = pass_on(buf, mod4(x + 1), 1, 64, dev(dx=3))
        return [sent[1, 1], sent[3, 0], a, b]

    class Head:
        def __init__(self, buf, rows):
            self.buf, self.rows = buf, rows
            self.zs, self.ys, self.last = {}, {}, []

        def z_start(self, which):
            for d, h in which:
                self.zs[d, h] = pass_on(self.buf, piece, h, self.rows, dev(dzh=d))

        def z_forward(self):
            self.zf = {}
            for d, h, i in ((1, 0, prev * 4 + y), (3, 1, nxt * 4 + y)):
                arrive(self.zs[d, h])
                for k in (h * 2, h * 2 + 1):
                    self.zf[k] = pass_on(self.buf, i, k, self.rows // 2, dev(dzh=d))

        def far_start(self, k):
            arrive(self.zf[k])
            for d in (1, 3):
                self.ys["far", k, d] = pass_on(
                    self.buf, far * 4 + y, k, self.rows // 2, dev(dy=d)
                )

        def far_forward(self, k):
            d = 1 if k < 2 else 3
            arrive(self.ys["far", k, d])
            i = far * 4 + mod4(y - 1 if k < 2 else y + 1)
            self.last.append(pass_on(self.buf, i, k, self.rows // 2, dev(dy=d)))
            self.last.append(self.ys["far", k, 4 - d])

        def y_start(self, name, zi, h):
            for d in (1, 3):
                self.ys[name, h, d] = pass_on(
                    self.buf, zi * 4 + y, h, self.rows, dev(dy=d)
                )

        def y_forward(self, name, zi, h):
            d = 1 if h == 0 else 3
            arrive(self.ys[name, h, d])
            i = zi * 4 + mod4(y - 1 if h == 0 else y + 1)
            self.last.append(pass_on(self.buf, i, h, self.rows, dev(dy=d)))
            self.last.append(self.ys[name, h, 4 - d])

    prev, nxt, far = mod4(zh - 1), mod4(zh + 1), mod4(zh + 2)
    te = Head(bt_buf, 64)

    as_1 = x_start(as_hbm, as_buf)
    at_1 = x_start(at_hbm, at_buf)

    def y_direct(zi):
        ref = bs_buf.at[zi * 4 + y]
        return [send(ref, ref, dev(dy=d)) for d in (1, 3, 2)]

    arrive(*bs_a2a)
    st_z = [send(bs_buf.at[piece], bs_buf.at[piece], dev(dzh=d)) for d in (1, 3)]
    st_y = y_direct(zh)
    own_bt.wait()
    arrive(*bt_a2a)
    te.z_start(order[:2])
    te.y_start("own", zh, 0)
    te.y_start("own", zh, 1)
    as_2 = x_forward(as_1, as_buf)
    arrive(st_z[0])
    st_f = [pass_on(bs_buf, prev * 4 + y, 0, 32, dev(dzh=1))]
    arrive(st_z[1])
    st_f.append(pass_on(bs_buf, nxt * 4 + y, 1, 32, dev(dzh=3)))
    te.z_start(order[2:])
    st_y += y_direct(prev)
    st_y += y_direct(nxt)
    te.y_forward("own", zh, 0)
    te.y_forward("own", zh, 1)
    arrive(*st_f)
    st_y += y_direct(far)
    at_2 = x_forward(at_1, at_buf)
    te.z_forward()
    te.y_start("prev", prev, 0)
    te.y_start("next", nxt, 1)

    own_as.wait()
    arrive(*as_2)

    def turn(i, carry):
        cols = pl.ds(pl.multiple_of(i * 128, 128), 128)
        block = as_buf[:, :, cols].reshape(512, 128).astype(F32)
        flat = block.T.astype(BF16)
        for yy in range(4):
            at = pl.multiple_of((yy * 4 + i) * 32, 32)
            as_t[pl.ds(at, 32)] = flat[yy * 32 : (yy + 1) * 32]
        return carry

    lax.fori_loop(0, 4, turn, 0)

    te.y_forward("prev", prev, 0)
    te.y_forward("next", nxt, 1)
    arrive(te.zs[1, 1])
    te.y_start("prev", prev, 1)
    arrive(te.zs[3, 0])
    te.y_start("next", nxt, 0)
    arrive(*st_y)
    for i in range(16):
        tall = bs_buf[i].astype(F32).reshape(4, 2, 8, 256)
        rows = slice(i * 32, (i + 1) * 32)
        bs_full[rows, :256] = tall[:, 0].reshape(32, 256).astype(BF16)
        bs_full[rows, 256:] = tall[:, 1].reshape(32, 256).astype(BF16)

    def student_part(out, slot):
        out[...] = jnp.dot(as_buf[slot], bs_full[...], preferred_element_type=F32)

    cs_swap = []
    for k in range(2):
        student_part(cs_send.at[k], (1 - c) * 2 + k)
        cs_swap.append(send(cs_send.at[k], cs_recv.at[k], dev(dc=1)))
    for k in range(2):
        student_part(cs_own.at[k], c * 2 + k)

    def tokens_of(ref, chip):
        return ref.at[lax.div(chip, 2), pl.ds(pl.multiple_of(lax.rem(chip, 2) * 64, 64), 64)]

    def scatter_z(swaps, own, recv, zrecv):
        arrive(*swaps)
        copies = []
        for d in (2, 1, 3, 0):
            mine, theirs = tokens_of(own, mod4(zl + d)), tokens_of(recv, mod4(zl + d))
            mine[...] = mine[...] + theirs[...]
            if d > 0:
                copies.append(send(mine, zrecv.at[d - 1], dev(dzl=d)))
        return copies

    def teacher_part(out, slot, zi, first):
        a = at_buf[slot, :, pl.ds(pl.multiple_of(zi * 512, 512), 512)]
        b = bt_buf[pl.ds(zi * 4, 4)].reshape(512, 512)
        part = jnp.dot(a, b, preferred_element_type=F32)
        out[...] = part if first else out[...] + part

    def teacher_parts(zi, first):
        for k in range(2):
            teacher_part(ct_send.at[k], (1 - c) * 2 + k, zi, first)
            teacher_part(ct_own.at[k], c * 2 + k, zi, first)

    cs_z = scatter_z(cs_swap, cs_own, cs_recv, zs_recv)
    own_at.wait()
    arrive(*at_2)
    arrive(*te.last[:4])
    teacher_parts(zh, True)
    for k in (0, 2, 1, 3):
        te.far_start(k)
    te.y_forward("prev", prev, 1)
    te.y_forward("next", nxt, 0)
    for k in (0, 2, 1, 3):
        te.far_forward(k)
    arrive(*te.last[4:12])
    teacher_parts(prev, False)
    teacher_parts(nxt, False)
    arrive(*te.last[12:])

    ct_swap = []
    for k in range(2):
        teacher_part(ct_send.at[k], (1 - c) * 2 + k, far, False)
        ct_swap.append(send(ct_send.at[k], ct_recv.at[k], dev(dc=1)))
    for k in range(2):
        teacher_part(ct_own.at[k], c * 2 + k, far, False)
    ct_z = scatter_z(ct_swap, ct_own, ct_recv, zt_recv)
    drain()

    def scaled(own, zrecv):
        return (tokens_of(own, zl)[...] + zrecv[0] + zrecv[1] + zrecv[2]) * 0.5

    arrive(*cs_z)
    s = scaled(cs_own, zs_recv)
    ms = jnp.max(s, axis=-1, keepdims=True)
    es = jnp.sum(jnp.exp(s - ms), axis=-1, keepdims=True)
    arrive(*ct_z)
    t = scaled(ct_own, zt_recv)
    mt = jnp.max(t, axis=-1, keepdims=True)
    et = jnp.exp(t - mt)
    ws = jnp.sum(et * (t - s), axis=-1, keepdims=True)
    et = jnp.sum(et, axis=-1, keepdims=True)

    lane = lax.broadcasted_iota(jnp.int32, (64, 128), 1)
    stat = jnp.zeros((64, 128), F32)
    for i, col in enumerate((mt, et, ms, es, ws)):
        stat = jnp.where(lane == i, col, stat)
    flat = stat.T[:8]
    stat_buf[x] = jnp.concatenate([flat, flat], axis=1)
    stats = [send(stat_buf.at[x], stat_buf.at[x], dev(dx=d)) for d in (1, 3, 2)]
    arrive(*rests)
    arrive(*stats)
    got = [stat_buf[i] for i in range(4)]
    rests8 = rest_buf[c * 2 + lax.div(zl, 2)]

    def log_add(a, b):
        top = jnp.maximum(a, b)
        return top + jnp.log(jnp.exp(a - top) + jnp.exp(b - top))

    def whole(k):
        tops = [v[k : k + 1] for v in got]
        sums = [v[k + 1 : k + 2] for v in got]
        top = jnp.maximum(jnp.maximum(tops[0], tops[1]), jnp.maximum(tops[2], tops[3]))
        scale = [jnp.exp(m - top) for m in tops]
        total = sum(a * b for a, b in zip(sums, scale))
        return top, scale, total

    top_t, scale_t, sum_t = whole(0)
    top_s, _, sum_s = whole(2)
    norm_t = log_add(top_t + jnp.log(sum_t), rests8[0:1])
    norm_s = log_add(top_s + jnp.log(sum_s), rests8[1:2])
    upper = lax.rem(zl, 2)
    square = lax.broadcasted_iota(jnp.int32, (128, 128), 0)
    turned = jnp.where(square == 0, norm_t, norm_s).T
    turned = jnp.where(upper == 0, turned[:64], turned[64:])
    col_t, col_s = turned[:, 0:1], turned[:, 1:2]

    j = c * 4 + zl
    g_z, g_chip = [], []
    for v in range(2):
        cols = slice(v * 256, (v + 1) * 256)
        gap = jnp.exp(s[:, cols] - col_s) - jnp.exp(t[:, cols] - col_t)
        g_buf[v, j] = (8.0 * gap).astype(BF16)
        mine = g_buf.at[v, j]
        g_z.append([send(mine, mine, dev(dzl=d)) for d in (2, 1, 3)])
        g_chip.append(send(mine, mine, dev(dc=1)))

    weighted = sum(v[4:5] * b for v, b in zip(got, scale_t))
    inside = jnp.exp(top_t - norm_t)
    kl = 16.0 * (weighted * inside - sum_t * inside * (norm_t - norm_s))
    half_of = lax.div(lax.broadcasted_iota(jnp.int32, (1, 128), 1), 64)
    kl_buf[j] = jnp.broadcast_to(jnp.where(half_of == upper, kl, 0.0), (8, 128))
    kls = [
        send(kl_buf.at[j], kl_buf.at[j], dev(dzl=a, dc=b))
        for a in range(4)
        for b in range(2)
        if a + b > 0
    ]

    gw_c, gh_c = [], []
    for v in range(2):
        g_f = []
        for copy, d in zip(g_z[v], (2, 1, 3)):
            arrive(copy)
            theirs = g_buf.at[v, c * 4 + mod4(zl - d)]
            g_f.append(send(theirs, theirs, dev(dc=1)))
        arrive(g_chip[v], *g_f)

        g = g_buf[v].reshape(512, 256)
        sent = []
        for d in (2, 1, 3, 0):
            rows = pl.ds(pl.multiple_of(mod4(y + d) * 128, 128), 128)
            part = jnp.dot(as_t[rows], g, preferred_element_type=F32)
            if d == 0:
                gw_own[v] = part
            else:
                gw_send[v, d - 1] = part.astype(BF16)
                sent.append(send(gw_send.at[v, d - 1], gw_recv.at[v, d - 1], dev(dy=d)))
        gw_c.append(sent)

        for d in (2, 1, 3, 0):
            rows = g_buf[v, pl.ds(mod4(x + d) * 2, 2)].reshape(128, 256)
            part = lax.dot_general(
                rows,
                bs_full[:, v * 256 : (v + 1) * 256],
                (((1,), (1,)), ((), ())),
                preferred_element_type=F32,
            )
            if v == 0:
                gh_own[d] = part
            elif d == 0:
                gh_own[0] = gh_own[0] + part
            else:
                gh_send[d - 1] = (gh_own[d] + part).astype(BF16)
                gh_c.append(send(gh_send.at[d - 1], gh_recv.at[d - 1], dev(dx=d)))

    w_c = []
    for v in range(2):
        arrive(*gw_c[v])
        total = gw_own[v] + sum(gw_recv[v, k].astype(F32) for k in range(3))
        total = total.reshape(4, 32, 256)
        w_own[v] = total
        w_send[v] = total.astype(BF16)
        w_c.append(
            [
                send(w_send.at[v, mod4(zh + d)], w_recv.at[v, d - 1], dev(dzh=d))
                for d in (2, 1, 3)
            ]
        )

    def write_out(src, dst, k):
        copy = pltpu.make_async_copy(src, dst, local_sem.at[k])
        copy.start()
        return copy

    arrive(*gh_c)
    gh_vmem[...] = gh_own[0] + sum(gh_recv[k].astype(F32) for k in range(3))
    outs = [write_out(gh_vmem, gh_out, 6)]
    arrive(*kls)
    k0 = lax.div(x, 2) * 4 + lax.rem(x, 2) * 2
    kl_vmem[...] = kl_buf[k0, 0:1] + kl_buf[k0 + 1, 0:1]
    outs.append(write_out(kl_vmem, kl_out, 7))

    x_c = []
    for v in range(2):
        arrive(*w_c[v])
        rows = w_own[v, zh] + sum(w_recv[v, k].astype(F32) for k in range(3))
        x_send[v] = rows.reshape(4, 8, 256)
        cols = pl.ds(pl.multiple_of(x * 512 + v * 256, 256), 256)
        gw_vmem[:, cols] = x_send[v, x]
        x_c += [
            send(x_send.at[v, mod4(x + d)], gw_vmem.at[:, cols], dev(dx=d))
            for d in (2, 1, 3)
        ]
    drain()
    arrive(*x_c)
    outs.append(write_out(gw_vmem, gw_out, 8))
    for copy in outs:
        copy.wait()


def settle_kernel(kl_in, gw_in, gh_in, kl_out, gw_out, gh_out, kl_vmem, gw_vmem, gh_vmem, sem):
    ways = ((gh_in, gh_vmem, gh_out), (gw_in, gw_vmem, gw_out), (kl_in, kl_vmem, kl_out))
    into = [pltpu.make_async_copy(a, b, sem.at[i]) for i, (a, b, _) in enumerate(ways)]
    onto = [pltpu.make_async_copy(b, o, sem.at[3 + i]) for i, (_, b, o) in enumerate(ways)]
    for copy in into:
        copy.start()
    for first, then in zip(into, onto):
        first.wait()
        then.start()
    for copy in onto:
        copy.wait()


def body(teacher_hidden, teacher_head, student_hidden, student_head, teacher_rest, student_rest):
    hbm = pl.BlockSpec(memory_space=pltpu.HBM)
    out_shape = (
        jax.ShapeDtypeStruct((1, 128), F32),
        jax.ShapeDtypeStruct((8, 2048), F32),
        jax.ShapeDtypeStruct((128, 512), F32),
    )
    results = pl.pallas_call(
        distill_kernel,
        out_shape=out_shape,
        in_specs=[hbm] * 6,
        out_specs=(hbm, hbm, hbm),
        scratch_shapes=[
            pltpu.VMEM((8, 2048), BF16),
            pltpu.VMEM((1, 128), F32),
            pltpu.VMEM((1, 128), F32),
            pltpu.VMEM((4, 16, 256), BF16),
            pltpu.VMEM((8, 128), F32),
            pltpu.VMEM((4, 128, 2048), BF16),
            pltpu.VMEM((4, 128, 512), BF16),
            pltpu.VMEM((16, 128, 512), BF16),
            pltpu.VMEM((16, 64, 256), BF16),
            pltpu.VMEM((512, 512), BF16),
            pltpu.VMEM((512, 512), BF16),
            pltpu.VMEM((4, 8, 128), F32),
            pltpu.VMEM((2, 128, 512), F32),
            pltpu.VMEM((2, 128, 512), F32),
            pltpu.VMEM((2, 128, 512), F32),
            pltpu.VMEM((2, 128, 512), F32),
            pltpu.VMEM((2, 128, 512), F32),
            pltpu.VMEM((2, 128, 512), F32),
            pltpu.VMEM((3, 64, 512), F32),
            pltpu.VMEM((3, 64, 512), F32),
            pltpu.VMEM((4, 8, 128), F32),
            pltpu.VMEM((2, 8, 64, 256), BF16),
            pltpu.VMEM((8, 8, 128), F32),
            pltpu.VMEM((4, 128, 512), F32),
            pltpu.VMEM((3, 128, 512), BF16),
            pltpu.VMEM((3, 128, 512), BF16),
            pltpu.VMEM((2, 128, 256), F32),
            pltpu.VMEM((2, 3, 128, 256), BF16),
            pltpu.VMEM((2, 3, 128, 256), BF16),
            pltpu.VMEM((2, 4, 32, 256), F32),
            pltpu.VMEM((2, 4, 32, 256), BF16),
            pltpu.VMEM((2, 3, 32, 256), BF16),
            pltpu.VMEM((2, 4, 8, 256), F32),
            pltpu.VMEM((1, 128), F32),
            pltpu.VMEM((8, 2048), F32),
            pltpu.VMEM((128, 512), F32),
            pltpu.SemaphoreType.DMA((N_COPY,)),
            pltpu.SemaphoreType.DMA((N_COPY,)),
            pltpu.SemaphoreType.DMA((9,)),
        ],
        compiler_params=pltpu.CompilerParams(
            collective_id=0, has_side_effects=True, vmem_limit_bytes=63 * 1024 * 1024
        ),
    )(
        teacher_hidden,
        teacher_head,
        student_hidden,
        student_head,
        teacher_rest.reshape(1, 128),
        student_rest.reshape(1, 128),
    )
    kl, grad_head, grad_hidden = pl.pallas_call(
        settle_kernel,
        out_shape=out_shape,
        in_specs=[hbm] * 3,
        out_specs=(hbm, hbm, hbm),
        scratch_shapes=[
            pltpu.VMEM((1, 128), F32),
            pltpu.VMEM((8, 2048), F32),
            pltpu.VMEM((128, 512), F32),
            pltpu.SemaphoreType.DMA((6,)),
        ],
        compiler_params=pltpu.CompilerParams(vmem_limit_bytes=63 * 1024 * 1024),
    )(*results)
    return kl.reshape(128), grad_head, grad_hidden


def solution(mesh):
    return jax.shard_map(
        body,
        mesh=mesh,
        in_specs=(
            P("fsdp", "role"),
            P(("role", "fsdp"), None),
            P("fsdp", "role"),
            P(("role", "fsdp"), None),
            P("fsdp"),
            P("fsdp"),
        ),
        out_specs=(P("fsdp"), P(("role", "fsdp"), None), P("fsdp", "role")),
        check_vma=False,
    )
```
